128 devices in a mesh: row: 16 (over x, y_lo, core), col: 8 (over y_hi, z).
Axes of the slice: x: 4, y: 4 (y_hi: 2, y_lo: 2; y = y_hi * 2 + y_lo), z: 4, core: 2. Of those that a mesh axis runs over, the one named last changes fastest.
Arguments:
- a_values: bfloat16 [8192, 8192], P('row', 'col'), may hold values from -0.15625 to 0.15625
- b_values: bfloat16 [8192, 8192], P('row', 'col'), may hold values from -6 to 6
- a_pattern: int32 [64, 64], P('row', 'col'), may hold values from 0 to 1, as said below
- b_pattern: int32 [64, 64], P('row', 'col'), may hold values from 0 to 1, as said below
- c_pattern: int32 [64, 64], P('row', 'col'), may hold values from 0 to 1, as said below
- owner_list: int32 [64], replicated, may hold values from 0 to 63, as said below
Outputs:
- product: bfloat16 [8192, 8192], P('row', 'col')
The draws below stay inside these ranges and needn't reach their ends.
Inputs may be any that keep to these rules, and one draw needn't show every extreme that they name: a_pattern is 0 or 1 for each block. b_pattern is 0 or 1 for each block. c_pattern is 0 or 1 for each block. owner_list is a permutation of 0 to 63 of the form owner_list[d * 4 + s] = ((d + shift_s) mod 16) * 4 + q_s, with q a permutation of the 4 slots, slots 2p and 2p+1 sharing one shift, the shifts of different pairs distinct and none zero.
All inputs are finite; a program needn't handle non-finite values.
Results may differ from the reference program's by a relative error of at most 0.001.
Values may be sent and summed in bfloat16 or wider, within the bound.
No kernel may reach another device: no remote copies, remote signals or barrier semaphores. Data moves between devices by JAX's collectives and lax.ppermute only.
A program may use at most 128 MiB of HBM per device.

```python
import jax
import jax.numpy as jnp

BLK = 128
BR = 4
NB = 64
N = 8192
N_ROW = 16


def banded_mask(key, reach):
    index = jnp.arange(NB, dtype=jnp.int32)
    distance = jnp.abs(index[:, None] - index[None, :])
    scattered = jax.random.randint(key, (NB, NB), 0, 32) == 0
    kept = jnp.logical_or(distance <= reach, scattered)
    return kept.astype(jnp.int32)


def draw_a_pattern(key, part):
    key = jax.random.fold_in(key, 11)
    return banded_mask(key, max(1, NB // 10))


def draw_b_pattern(key, part):
    key = jax.random.fold_in(key, 13)
    return banded_mask(key, max(1, NB // 10))


def draw_c_pattern(key, part):
    key = jax.random.fold_in(key, 17)
    return banded_mask(key, max(2, NB // 5))


def draw_owner_list(key, part):
    key = jax.random.fold_in(key, 7)
    first, second = jax.random.split(key)
    slots = jax.random.permutation(first, BR)
    shifts = 1 + jax.random.permutation(second, N_ROW - 1)[:BR // 2]
    slot_shift = jnp.repeat(shifts, 2)
    dest = jnp.arange(N_ROW, dtype=jnp.int32)[:, None]
    source = (dest + slot_shift[None, :]) % N_ROW
    listed = source * BR + slots[None, :]
    return listed.reshape(NB).astype(jnp.int32)


def levels(key, shape, cuts, low, high):
    gain, own = 1.0, jax.random.fold_in(key, 6)
    for axis_at, blocks in cuts:
        heights = jnp.exp(jax.random.uniform(jax.random.fold_in(own, axis_at), (blocks,), jnp.float32, low / len(cuts), high / len(cuts)))
        gain = gain * jnp.repeat(heights, shape[axis_at] // blocks).reshape([-1 if axis == axis_at else 1 for axis in range(len(shape))])
    return gain


def centred(own_key, extent, deviation, limit, pieces=(), kind=jnp.bfloat16):
    values = deviation * jax.random.normal(own_key, extent, jnp.float32)
    if pieces:
        values = values * levels(own_key, extent, pieces, -0.22, 0.18)
    return jnp.clip(values, -limit, limit).astype(kind)


def setup_inputs(seed: int = 0) -> dict:
    seeds = jax.random.split(jax.random.key(seed), 7)
    return {
        "a_values": centred(seeds[0], (N, N), (N // 5) ** -0.5, 0.15625, ((0, 16), (1, 8))),
        "b_values": centred(seeds[1], (N, N), 1.0, 6.0, ((0, 16), (1, 8))),
        "a_pattern": draw_a_pattern(jax.random.fold_in(seeds[6], 71), 0),
        "b_pattern": draw_b_pattern(jax.random.fold_in(seeds[6], 71), 0),
        "c_pattern": draw_c_pattern(jax.random.fold_in(seeds[6], 71), 0),
        "owner_list": draw_owner_list(jax.random.fold_in(seeds[6], 71), 0),
    }


def expand(pattern, width):
    grown = jnp.repeat(jnp.repeat(pattern, width, axis=0), width, axis=1)
    return grown


def reference(a_values, b_values, a_pattern, b_pattern, c_pattern, owner_list):
    masked_a = jnp.where(expand(a_pattern, BLK) > 0, a_values, jnp.zeros_like(a_values))
    masked_b = jnp.where(expand(b_pattern, BLK) > 0, b_values, jnp.zeros_like(b_values))
    full = jnp.dot(masked_a, masked_b, preferred_element_type=jnp.float32)
    full = jnp.where(expand(c_pattern, BLK) > 0, full, jnp.float32(0.0))
    blocks = full.reshape(NB, BLK, N)
    moved = blocks[owner_list.astype(jnp.int32)]
    return moved.reshape(N, N).astype(jnp.bfloat16)
```

```python
import jax
import jax.numpy as jnp
from jax import lax
from jax.sharding import PartitionSpec as P


def expand(pattern, width):
    return jnp.repeat(jnp.repeat(pattern, width, axis=0), width, axis=1)


def shifted(value, axis, shift):
    count = lax.axis_size(axis)

    def branch(by):
        return lambda v: lax.ppermute(v, axis, [((i + by) % count, i) for i in range(count)])

    return lax.switch(shift - 1, [branch(by) for by in range(1, count)], value)


def local(a_values, b_values, a_pattern, b_pattern, c_pattern, owner_list):
    width = a_values.shape[0] // a_pattern.shape[0]
    masked_a = jnp.where(expand(a_pattern, width) > 0, a_values, jnp.zeros_like(a_values))
    masked_b = jnp.where(expand(b_pattern, width) > 0, b_values, jnp.zeros_like(b_values))
    local_cols = b_values.shape[1]
    b_panel = lax.all_gather(masked_b, "row", axis=0, tiled=True)
    full = jnp.dot(
        lax.all_gather(masked_a, "col", axis=1, tiled=True),
        b_panel,
        preferred_element_type=jnp.float32,
    )
    full = jnp.where(expand(c_pattern, width) > 0, full, jnp.float32(0.0))
    rounded = full.astype(jnp.bfloat16)
    row_count = lax.axis_size("row")
    blocks_here = a_pattern.shape[0]
    slot_shift = owner_list[:blocks_here] // blocks_here % row_count
    slot_source = owner_list[:blocks_here] % blocks_here
    out = []
    for pair in range(blocks_here // 2):
        rows = [lax.dynamic_slice_in_dim(rounded, slot_source[2 * pair + t] * width, width, 0) for t in range(2)]
        out.append(shifted(jnp.concatenate(rows, axis=0), "row", slot_shift[2 * pair]))
    return jnp.concatenate(out, axis=0)


def solution(mesh):
    return jax.shard_map(
        local,
        mesh=mesh,
        in_specs=(
            P("row", "col"),
            P("row", "col"),
            P("row", "col"),
            P("row", "col"),
            P("row", "col"),
            P(),
        ),
        out_specs=P("row", "col"),
        check_vma=False,
    )
```

```python
import jax
import jax.numpy as jnp
import numpy as np
from jax import lax
from jax.experimental import pallas as pl
from jax.experimental.pallas import tpu as pltpu
from jax.sharding import Mesh, PartitionSpec as P

SIZES = {"x": 4, "yl": 2, "core": 2, "yh": 2, "z": 4}
ROW = ("x", "yl", "core")
COL = ("yh", "z")
WIDTH = 128


def shifted(values, axis, count, shift):
    def branch(by):
        perm = [((i + by) % count, i) for i in range(count)]
        return lambda vs: tuple(lax.ppermute(v, axis, perm) for v in vs)

    return lax.switch(shift - 1, [branch(by) for by in range(1, count)], tuple(values))


def from_ahead(value, axis, by):
    n = SIZES[axis]
    return lax.ppermute(value, axis, [((i + by) % n, i) for i in range(n)])


def mask_a_kernel(slots, pattern, a_ref, *outs):
    for slot in range(4):
        source = slots[slot]
        for j in range(8):
            rows = pl.ds(pl.multiple_of(source * WIDTH, WIDTH), WIDTH)
            block = a_ref[rows, j * WIDTH : (j + 1) * WIDTH]
            outs[slot // 2][(slot % 2) * WIDTH : (slot % 2 + 1) * WIDTH, j * WIDTH : (j + 1) * WIDTH] = jnp.where(
                pattern[source, j] > 0, block, jnp.zeros_like(block)
            )


def mask_b_kernel(pattern, b_ref, *outs):
    per = 8 // len(outs)
    for i in range(4):
        for j in range(8):
            block = b_ref[i * WIDTH : (i + 1) * WIDTH, j * WIDTH : (j + 1) * WIDTH]
            at = j % per
            outs[j // per][i * WIDTH : (i + 1) * WIDTH, at * WIDTH : (at + 1) * WIDTH] = jnp.where(
                pattern[i, j] > 0, block, jnp.zeros_like(block)
            )


def vmem():
    return pl.BlockSpec(memory_space=pltpu.VMEM)


def smem():
    return pl.BlockSpec(memory_space=pltpu.SMEM)


def local(a, b, a_pattern, b_pattern, c_pattern, owner_list):
    slot_shift = owner_list[:4] // 4 % 16
    slot_source = owner_list[:4] % 4
    halves = 2
    b_parts = pl.pallas_call(
        mask_b_kernel,
        in_specs=[smem(), vmem()],
        out_specs=[vmem()] * halves,
        out_shape=[jax.ShapeDtypeStruct((512, 1024 // halves), jnp.bfloat16)] * halves,
    )(b_pattern, b)
    a_pairs = pl.pallas_call(
        mask_a_kernel,
        in_specs=[smem(), smem(), vmem()],
        out_specs=[vmem()] * 2,
        out_shape=[jax.ShapeDtypeStruct((256, 1024), jnp.bfloat16)] * 2,
    )(slot_source, a_pattern, a)
    panels = [lax.all_gather(part, ROW, axis=0, tiled=True) for part in b_parts]

    rows, kept = [], []
    for pair in range(2):
        flags = jnp.stack([lax.dynamic_index_in_dim(c_pattern, slot_source[2 * pair + t], 0, False) for t in range(2)])
        moved, flags = shifted((a_pairs[pair], flags), ROW, 16, slot_shift[2 * pair])
        rows.append(moved)
        kept.append(flags)
    own = jnp.concatenate(rows, axis=0)
    kept = jnp.concatenate(kept, axis=0)

    yh, z = lax.axis_index("yh"), lax.axis_index("z")
    full = jnp.zeros((512, 8192), jnp.bfloat16)

    def place(full, piece, dy, dz, top=0):
        at = ((yh + dy) % 2 * 4 + (z + dz) % 4) * 1024
        return lax.dynamic_update_slice(full, piece, (top, at))

    other = from_ahead(own, "yh", 1)
    for dy, value in ((0, own), (1, other)):
        ahead = from_ahead(value, "z", 1)
        behind = from_ahead(value, "z", -1)
        far_top = from_ahead(ahead[:256], "z", 1)
        far_low = from_ahead(behind[256:], "z", -1)
        full = place(full, value, dy, 0)
        full = place(full, ahead, dy, 1)
        full = place(full, behind, dy, -1)
        full = place(full, far_top, dy, 2)
        full = place(full, far_low, dy, 2, 256)

    out = []
    for h, panel in enumerate(panels):
        part = jnp.dot(full, panel, preferred_element_type=jnp.float32)
        per = 8 // halves
        mask = jnp.repeat(jnp.repeat(kept[:, h * per : (h + 1) * per], WIDTH, axis=0), WIDTH, axis=1)
        out.append(jnp.where(mask > 0, part, jnp.float32(0.0)).astype(jnp.bfloat16))
    return jnp.concatenate(out, axis=1)


def solution(mesh):
    fine = Mesh(mesh.devices.reshape(tuple(SIZES.values())), tuple(SIZES))
    return jax.shard_map(
        local,
        mesh=fine,
        in_specs=(P(ROW, COL),) * 5 + (P(),),
        out_specs=P(ROW, COL),
        check_vma=False,
    )
```

```python
import jax
import jax.numpy as jnp
from jax import lax
from jax.experimental import pallas as pl
from jax.experimental.pallas import tpu as pltpu
from jax.sharding import Mesh, PartitionSpec as P

SIZES = {"x": 4, "yl": 2, "core": 2, "yh": 2, "z": 4}
ROW = ("x", "yl", "core")
COL = ("yh", "z")
WIDTH = 128
HALVES = 1


def from_ahead(value, axis, by):
    n = SIZES[axis]
    return lax.ppermute(value, axis, [((i + by) % n, i) for i in range(n)])


def shifted(value, axis, count, shift):
    def branch(by):
        perm = [((i + by) % count, i) for i in range(count)]
        return lambda v: lax.ppermute(v, axis, perm)

    return lax.switch(shift - 1, [branch(by) for by in range(1, count)], value)


def mask_kernel(pattern, ref, *outs):
    per = 8 // len(outs)
    for i in range(4):
        for j in range(8):
            block = ref[i * WIDTH : (i + 1) * WIDTH, j * WIDTH : (j + 1) * WIDTH]
            at = j % per
            outs[j // per][i * WIDTH : (i + 1) * WIDTH, at * WIDTH : (at + 1) * WIDTH] = jnp.where(
                pattern[i, j] > 0, block, jnp.zeros_like(block)
            )


def masked(value, pattern, parts):
    out = jax.ShapeDtypeStruct((512, 1024 // parts), jnp.bfloat16)
    vmem = pl.BlockSpec(memory_space=pltpu.VMEM)
    return pl.pallas_call(
        mask_kernel,
        in_specs=[pl.BlockSpec(memory_space=pltpu.SMEM), vmem],
        out_specs=[vmem] * parts,
        out_shape=[out] * parts,
    )(pattern, value)


def local(a, b, a_pattern, b_pattern, c_pattern, owner_list):
    slot_shift = owner_list[:4] // 4 % 16
    slot_source = owner_list[:4] % 4
    yh, z = lax.axis_index("yh").astype(jnp.int32), lax.axis_index("z").astype(jnp.int32)
    own_b = masked(b, b_pattern, HALVES)
    panels = [lax.all_gather(part, ROW, axis=0, tiled=True) for part in own_b]
    (own_a,) = masked(a, a_pattern, 1)

    full = jnp.zeros((512, 8192), jnp.bfloat16)

    def place(full, piece, dy, step, top=0):
        at = ((yh + dy) % 2 * 4 + (z + step) % 4) * 1024
        return lax.dynamic_update_slice(full, piece, (top, at))

    ahead, behind = from_ahead(own_a, "z", 1), from_ahead(own_a, "z", -1)
    side = from_ahead(own_a, "yh", 1)
    side_ahead, side_behind = from_ahead(side, "z", 1), from_ahead(side, "z", -1)
    for dy, value, up, down in ((0, own_a, ahead, behind), (1, side, side_ahead, side_behind)):
        full = place(full, value, dy, 0)
        full = place(full, up, dy, 1)
        full = place(full, down, dy, -1)
        full = place(full, from_ahead(up[:256], "z", 1), dy, 2)
        full = place(full, from_ahead(down[256:], "z", -1), dy, 2, 256)

    out = []
    per = 8 // HALVES
    for h, panel in enumerate(panels):
        part = jnp.dot(full, panel, preferred_element_type=jnp.float32)
        mask = jnp.repeat(jnp.repeat(c_pattern[:, h * per : (h + 1) * per], WIDTH, axis=0), WIDTH, axis=1)
        part = jnp.where(mask > 0, part, jnp.float32(0.0)).astype(jnp.bfloat16)
        moved = []
        for pair in range(2):
            rows = [lax.dynamic_slice_in_dim(part, slot_source[2 * pair + t] * WIDTH, WIDTH, 0) for t in range(2)]
            moved.append(shifted(jnp.concatenate(rows, axis=0), ROW, 16, slot_shift[2 * pair]))
        out.append(jnp.concatenate(moved, axis=0))
    return out[0] if HALVES == 1 else jnp.concatenate(out, axis=1)


def solution(mesh):
    fine = Mesh(mesh.devices.reshape(tuple(SIZES.values())), tuple(SIZES))
    return jax.shard_map(
        local,
        mesh=fine,
        in_specs=(P(ROW, COL),) * 5 + (P(),),
        out_specs=P(ROW, COL),
        check_vma=False,
    )
```

```python
import jax
import jax.numpy as jnp
from jax import lax
from jax.experimental import pallas as pl
from jax.experimental.pallas import tpu as pltpu
from jax.sharding import Mesh, PartitionSpec as P

SIZES = {"x": 4, "yl": 2, "core": 2, "yh": 2, "z": 4}
ROW = ("x", "yl", "core")
COL = ("yh", "z")
WIDTH = 128
SLICE = 16
CAP = 40
PIECE = 33 * SLICE
PACKED = (CAP + 1) * SLICE
CHUNK = 4
OFFSETS = [(dy, dz) for dy in range(2) for dz in range(4)]


def space(kind):
    return pl.BlockSpec(memory_space=kind)


def from_ahead(value, axis, by):
    n = SIZES[axis]
    return lax.ppermute(value, axis, [((i + by) % n, i) for i in range(n)])


def from_offset(value, offset):
    return lax.ppermute(
        value,
        COL,
        [((y + offset[0]) % 2 * 4 + (z + offset[1]) % 4, y * 4 + z) for y in range(2) for z in range(4)],
    )


def shifted(value, axis, count, shift):
    def branch(by):
        perm = [((i + by) % count, i) for i in range(count)]
        return lambda v: lax.ppermute(v, axis, perm)

    return lax.switch(shift - 1, [branch(by) for by in range(1, count)], value)


def mask_kernel(pattern, ref, out):
    for i in range(4):
        for j in range(8):
            at = (slice(i * WIDTH, (i + 1) * WIDTH), slice(j * WIDTH, (j + 1) * WIDTH))
            block = ref[at]
            out[at] = jnp.where(pattern[i, j] > 0, block, jnp.zeros_like(block))


def masked(value, pattern):
    return pl.pallas_call(
        mask_kernel,
        in_specs=[space(pltpu.SMEM), space(pltpu.VMEM)],
        out_specs=space(pltpu.VMEM),
        out_shape=jax.ShapeDtypeStruct((512, 1024), jnp.bfloat16),
    )(pattern, value)


def flags_as_rows(flags, lane):
    row = jnp.zeros((SLICE, WIDTH), jnp.float32)
    for i in range(4):
        for j in range(8):
            row = jnp.where(lane == i * 8 + j, flags[i, j].astype(jnp.float32), row)
    return row


def cut_kernel(pattern, ref, out):
    lane = lax.broadcasted_iota(jnp.int32, (SLICE, WIDTH), 1)
    row = flags_as_rows(pattern, lane).astype(jnp.bfloat16)
    for m in range(8):
        for i in range(4):
            rows = slice(i * WIDTH + m * SLICE, i * WIDTH + (m + 1) * SLICE)
            for j in range(8):
                at = PIECE * m + (i * 8 + j) * SLICE
                out[at : at + SLICE] = ref[rows, j * WIDTH : (j + 1) * WIDTH]
        out[PIECE * m + 32 * SLICE : PIECE * (m + 1)] = row


def cut(value, pattern):
    return pl.pallas_call(
        cut_kernel,
        in_specs=[space(pltpu.SMEM), space(pltpu.VMEM)],
        out_specs=space(pltpu.VMEM),
        out_shape=jax.ShapeDtypeStruct((8 * PIECE, WIDTH), jnp.bfloat16),
    )(pattern, value)


def pack_a_kernel(slots, c_pattern, pieces, first, second, most, flags_v, flags_s, place_s, sem):
    packed = (first, second)
    for m in range(8):
        row = pieces[PIECE * m + 32 * SLICE : PIECE * (m + 1)].astype(jnp.float32).astype(jnp.int32)
        flags_v[m : m + 1] = row[0:1]
    copy = pltpu.make_async_copy(flags_v, flags_s, sem)
    copy.start()
    copy.wait()
    counts = []
    for pair in range(2):
        count = jnp.int32(0)
        for slot in range(2):
            q = slots[2 * pair + slot]

            def step(k, count, pair=pair, q=q):
                at = q * 8 + k % 8
                here = flags_s[k // 8, at]
                to = jnp.minimum(count, CAP)
                packed[pair][pl.ds(pl.multiple_of(to * SLICE, SLICE), SLICE)] = pieces[
                    pl.ds(pl.multiple_of(k // 8 * PIECE + at * SLICE, SLICE), SLICE)
                ]
                place_s[k // 8, at] = jnp.where(here > 0, to + 1, 0)
                return count + jnp.where(here > 0, 1, 0)

            count = lax.fori_loop(0, 64, step, count, unroll=8)
        counts.append(count)
    copy = pltpu.make_async_copy(place_s, flags_v, sem)
    copy.start()
    copy.wait()
    lane = lax.broadcasted_iota(jnp.int32, (SLICE, WIDTH), 1)
    sub = lax.broadcasted_iota(jnp.int32, (SLICE, WIDTH), 0)
    kept = flags_as_rows(c_pattern, lane)
    place = flags_v[...].astype(jnp.float32)
    place = jnp.where(lane < 32, jnp.concatenate([place, place], axis=0), jnp.float32(0.0))
    header = jnp.where(sub < 8, place, kept).astype(jnp.bfloat16)
    for ref in packed:
        ref[CAP * SLICE : (CAP + 1) * SLICE] = header
    most[...] = jnp.full((8, WIDTH), jnp.maximum(counts[0], counts[1]), jnp.int32)


def pack_a(pieces, slots, c_pattern):
    out = jax.ShapeDtypeStruct((PACKED, WIDTH), jnp.bfloat16)
    return pl.pallas_call(
        pack_a_kernel,
        in_specs=[space(pltpu.SMEM)] * 2 + [space(pltpu.VMEM)],
        out_specs=[space(pltpu.VMEM)] * 3,
        out_shape=[out, out, jax.ShapeDtypeStruct((8, WIDTH), jnp.int32)],
        scratch_shapes=[
            pltpu.VMEM((8, WIDTH), jnp.int32),
            pltpu.SMEM((8, WIDTH), jnp.int32),
            pltpu.SMEM((8, WIDTH), jnp.int32),
            pltpu.SemaphoreType.DMA,
        ],
    )(slots, c_pattern, pieces)


def product_kernel(source, slots, *refs):
    parts, panel, out = refs[:4], refs[4], refs[5]
    header_v, header_s, listed, rhs, lhs, total, sem, b_sem = refs[6:]
    for pair in range(2):
        at = pair * PACKED + CAP * SLICE
        header_v[pair * SLICE : (pair + 1) * SLICE] = parts[0][at : at + SLICE].astype(jnp.float32).astype(jnp.int32)
    copy = pltpu.make_async_copy(header_v, header_s, sem)
    copy.start()
    copy.wait()

    length = jnp.int32(0)
    chunks = []
    for pair in range(2):
        q0, q1 = slots[2 * pair], slots[2 * pair + 1]

        def step(k, length, pair=pair, q0=q0, q1=q1):
            first = header_s[pair * SLICE + k // 8, q0 * 8 + k % 8]
            second = header_s[pair * SLICE + k // 8, q1 * 8 + k % 8]
            listed[0, length] = k
            listed[1, length] = first
            listed[2, length] = second
            return length + jnp.where(first + second > 0, 1, 0)

        length = lax.fori_loop(0, 64, step, length, unroll=8)
        for i in range(CHUNK - 1):
            for n in range(3):
                listed[n, length + i] = 0
        length = (length + CHUNK - 1) // CHUNK * CHUNK
        chunks.append(length // CHUNK)
    total[...] = jnp.zeros_like(total)

    def b_copies(chunk):
        slot = chunk % 2
        return [
            pltpu.make_async_copy(
                panel.at[pl.ds(pl.multiple_of(listed[0, chunk * CHUNK + i] * WIDTH, WIDTH), WIDTH)],
                rhs.at[slot, pl.ds(i * WIDTH, WIDTH)],
                b_sem.at[slot, i],
            )
            for i in range(CHUNK)
        ]

    @pl.when(chunks[1] > 0)
    def _():
        for copy in b_copies(jnp.int32(0)):
            copy.start()

    def multiply(chunk, carry):
        @pl.when(chunk + 1 < chunks[1])
        def _():
            for copy in b_copies(chunk + 1):
                copy.start()

        pair = jnp.where(chunk >= chunks[0], 1, 0)
        for i in range(CHUNK):
            for slot in range(2):
                place = listed[1 + slot, chunk * CHUNK + i]
                at = pair * PACKED + jnp.maximum(place - 1, 0) * SLICE
                for dy in range(2):
                    for step in range(4):
                        value = parts[step][pl.ds(pl.multiple_of(at + dy * 2 * PACKED, SLICE), SLICE)]
                        rows = pl.ds(pl.multiple_of(slot * WIDTH + source[dy * 4 + step] * SLICE, SLICE), SLICE)
                        lhs[rows, i * WIDTH : (i + 1) * WIDTH] = jnp.where(place > 0, value, jnp.zeros_like(value))
        for copy in b_copies(chunk):
            copy.wait()
        for n in range(4):
            cols = slice(n * 256, (n + 1) * 256)
            total[pair, :, cols] += jnp.dot(lhs[...], rhs[chunk % 2, :, cols], preferred_element_type=jnp.float32)
        return carry

    lax.fori_loop(0, chunks[1], multiply, 0)
    for slot in range(4):
        q = slots[slot]
        rows = slice(slot % 2 * WIDTH, (slot % 2 + 1) * WIDTH)
        for j in range(8):
            block = total[slot // 2, rows, j * WIDTH : (j + 1) * WIDTH]
            out[slot * WIDTH : (slot + 1) * WIDTH, j * WIDTH : (j + 1) * WIDTH] = jnp.where(
                header_s[slot // 2 * SLICE + 8, q * 8 + j] > 0, block, jnp.zeros_like(block)
            ).astype(jnp.bfloat16)


def packed_product(parts, panel, source, slots):
    return pl.pallas_call(
        product_kernel,
        in_specs=[space(pltpu.SMEM)] * 2 + [space(pltpu.VMEM)] * 4 + [space(pl.ANY)],
        out_specs=space(pltpu.VMEM),
        out_shape=jax.ShapeDtypeStruct((512, 1024), jnp.bfloat16),
        scratch_shapes=[
            pltpu.VMEM((2 * SLICE, WIDTH), jnp.int32),
            pltpu.SMEM((2 * SLICE, WIDTH), jnp.int32),
            pltpu.SMEM((3, 2 * 64 + 2 * CHUNK), jnp.int32),
            pltpu.VMEM((2, CHUNK * WIDTH, 1024), jnp.bfloat16),
            pltpu.VMEM((2 * WIDTH, CHUNK * WIDTH), jnp.bfloat16),
            pltpu.VMEM((2, 2 * WIDTH, 1024), jnp.float32),
            pltpu.SemaphoreType.DMA,
            pltpu.SemaphoreType.DMA((2, CHUNK)),
        ],
        compiler_params=pltpu.CompilerParams(vmem_limit_bytes=24 * 2**20),
    )(source, slots, *parts, panel)


def dense_product(a, a_pattern, c_pattern, panel, slots, slot_shift, source):
    value = masked(a, a_pattern)
    moved, kept = [], []
    for pair in range(2):
        rows = [lax.dynamic_slice_in_dim(value, slots[2 * pair + t] * WIDTH, WIDTH, 0) for t in range(2)]
        flags = [lax.dynamic_slice_in_dim(c_pattern, slots[2 * pair + t], 1, 0) for t in range(2)]
        moved.append(shifted(jnp.concatenate(rows, axis=0), ROW, 16, slot_shift[2 * pair]))
        kept.append(shifted(jnp.concatenate(flags, axis=0), ROW, 16, slot_shift[2 * pair]))
    value = jnp.concatenate(moved, axis=0)
    full = jnp.zeros((512, 8192), jnp.bfloat16)
    for t, offset in enumerate(OFFSETS):
        piece = from_offset(value, offset) if t else value
        full = lax.dynamic_update_slice(full, piece, (0, source[t] * 1024))
    product = jnp.dot(full, panel, preferred_element_type=jnp.float32)
    mask = jnp.repeat(jnp.repeat(jnp.concatenate(kept, axis=0), WIDTH, axis=0), WIDTH, axis=1)
    return jnp.where(mask > 0, product, jnp.float32(0.0)).astype(jnp.bfloat16)


def local(a, b, a_pattern, b_pattern, c_pattern, owner_list):
    slot_shift = owner_list[:4] // 4 % 16
    slots = owner_list[:4] % 4
    yh, z = lax.axis_index("yh").astype(jnp.int32), lax.axis_index("z").astype(jnp.int32)
    ahead = jnp.stack([(yh + dy) % 2 * 4 + (z + dz) % 4 for dy, dz in OFFSETS])
    own_b = masked(b, b_pattern)
    panel = lax.all_gather(own_b, ROW, axis=0, tiled=True)
    a, _ = lax.optimization_barrier((a, own_b))

    pieces = lax.all_to_all(cut(a, a_pattern), COL, 0, 0, tiled=True)
    first, second, most = pack_a(pieces, slots, c_pattern)
    for axis, by in (("x", 2), ("x", 1), ("yl", 1), ("core", 1)):
        most = jnp.maximum(most, from_ahead(most, axis, by))
    first = shifted(first, ROW, 16, slot_shift[0])
    second = shifted(second, ROW, 16, slot_shift[2])
    own = jnp.concatenate([first, second], axis=0)
    both = jnp.concatenate([own, from_ahead(own, "yh", 1)], axis=0)
    parts = [both] + [from_ahead(both, "z", step) for step in (1, 2, 3)]
    return lax.cond(
        most[0, 0] > CAP,
        lambda: dense_product(a, a_pattern, c_pattern, panel, slots, slot_shift, ahead),
        lambda: packed_product(parts, panel, ahead, slots),
    )


def solution(mesh):
    fine = Mesh(mesh.devices.reshape(tuple(SIZES.values())), tuple(SIZES))
    return jax.shard_map(
        local,
        mesh=fine,
        in_specs=(P(ROW, COL),) * 5 + (P(),),
        out_specs=P(ROW, COL),
        check_vma=False,
    )
```

```python
import functools

import jax
import jax.numpy as jnp
from jax import lax
from jax.experimental import pallas as pl
from jax.experimental.pallas import tpu as pltpu
from jax.sharding import Mesh, PartitionSpec as P

SIZES = {"x": 4, "yl": 2, "core": 2, "yh": 2, "z": 4}
ROW = ("x", "yl", "core")
COL = ("yh", "z")
WIDTH = 128
SLICE = 16
CAP = 40
PIECE = 33 * SLICE
PACKED = (CAP + 1) * SLICE
SLICE_B = 32
CAP_B = 42
PIECE_B = 32 * SLICE_B + SLICE
HEADER_B = CAP_B * SLICE_B
PACKED_B = HEADER_B + SLICE
CHUNK = 4
OFFSETS = [(dy, dz) for dy in range(2) for dz in range(4)]


def space(kind):
    return pl.BlockSpec(memory_space=kind)


def from_ahead(value, axis, by):
    n = SIZES[axis]
    return lax.ppermute(value, axis, [((i + by) % n, i) for i in range(n)])


def from_offset(value, offset):
    return lax.ppermute(
        value,
        COL,
        [((y + offset[0]) % 2 * 4 + (z + offset[1]) % 4, y * 4 + z) for y in range(2) for z in range(4)],
    )


def shifted(value, axis, count, shift):
    def branch(by):
        perm = [((i + by) % count, i) for i in range(count)]
        return lambda v: lax.ppermute(v, axis, perm)

    return lax.switch(shift - 1, [branch(by) for by in range(1, count)], value)


def shifted_both(value, shift):
    def branch(by):
        perms = [
            [((i + by) % 16 * 2 + (y + cross) % 2, i * 2 + y) for i in range(16) for y in range(2)] for cross in range(2)
        ]
        return lambda v: tuple(lax.ppermute(v, ROW + ("yh",), perm) for perm in perms)

    return lax.switch(shift - 1, [branch(by) for by in range(1, 16)], value)


def mask_kernel(pattern, ref, out):
    for i in range(4):
        for j in range(8):
            at = (slice(i * WIDTH, (i + 1) * WIDTH), slice(j * WIDTH, (j + 1) * WIDTH))
            block = ref[at]
            out[at] = jnp.where(pattern[i, j] > 0, block, jnp.zeros_like(block))


def masked(value, pattern):
    return pl.pallas_call(
        mask_kernel,
        in_specs=[space(pltpu.SMEM), space(pltpu.VMEM)],
        out_specs=space(pltpu.VMEM),
        out_shape=jax.ShapeDtypeStruct((512, 1024), jnp.bfloat16),
    )(pattern, value)


def flags_as_rows(flags, lane, first=0):
    row = jnp.zeros((SLICE, WIDTH), jnp.float32)
    for i in range(4):
        for j in range(8):
            row = jnp.where(lane == first + i * 8 + j, flags[i, j].astype(jnp.float32), row)
    return row


def cut_kernel(pattern, b_pattern, ref, out):
    lane = lax.broadcasted_iota(jnp.int32, (SLICE, WIDTH), 1)
    row = (flags_as_rows(pattern, lane) + flags_as_rows(b_pattern, lane, 32)).astype(jnp.bfloat16)
    for m in range(8):
        for i in range(4):
            rows = slice(i * WIDTH + m * SLICE, i * WIDTH + (m + 1) * SLICE)
            for j in range(8):
                at = PIECE * m + (i * 8 + j) * SLICE
                out[at : at + SLICE] = ref[rows, j * WIDTH : (j + 1) * WIDTH]
        out[PIECE * m + 32 * SLICE : PIECE * (m + 1)] = row


def cut(value, pattern, b_pattern):
    return pl.pallas_call(
        cut_kernel,
        in_specs=[space(pltpu.SMEM), space(pltpu.SMEM), space(pltpu.VMEM)],
        out_specs=space(pltpu.VMEM),
        out_shape=jax.ShapeDtypeStruct((8 * PIECE, WIDTH), jnp.bfloat16),
    )(pattern, b_pattern, value)


def cut_b_kernel(target, pattern, ref, *outs):
    lane = lax.broadcasted_iota(jnp.int32, (SLICE, WIDTH), 1)
    row = flags_as_rows(pattern, lane).astype(jnp.bfloat16)
    for n, out in enumerate(outs):
        for i in range(4):
            rows = pl.ds(pl.multiple_of(i * WIDTH + target[n] * SLICE_B, SLICE_B), SLICE_B)
            for j in range(8):
                at = (i * 8 + j) * SLICE_B
                out[at : at + SLICE_B] = ref[rows, j * WIDTH : (j + 1) * WIDTH]
        out[32 * SLICE_B : PIECE_B] = row


def cut_b(value, pattern, target):
    return pl.pallas_call(
        cut_b_kernel,
        in_specs=[space(pltpu.SMEM), space(pltpu.SMEM), space(pltpu.VMEM)],
        out_specs=[space(pltpu.VMEM)] * 4,
        out_shape=[jax.ShapeDtypeStruct((PIECE_B, WIDTH), jnp.bfloat16)] * 4,
    )(target, pattern, value)


def pack_a_kernel(slots, c_pattern, pieces, first, second, flags_v, flags_s, place_s, sem):
    packed = (first, second)
    for m in range(8):
        row = pieces[PIECE * m + 32 * SLICE : PIECE * (m + 1)].astype(jnp.float32).astype(jnp.int32)
        flags_v[m : m + 1] = row[0:1]
    copy = pltpu.make_async_copy(flags_v, flags_s, sem)
    copy.start()
    copy.wait()
    for pair in range(2):
        count = jnp.int32(0)
        for slot in range(2):
            q = slots[2 * pair + slot]

            def step(k, count, pair=pair, q=q):
                at = q * 8 + k % 8
                here = flags_s[k // 8, at]
                to = jnp.minimum(count, CAP)
                packed[pair][pl.ds(pl.multiple_of(to * SLICE, SLICE), SLICE)] = pieces[
                    pl.ds(pl.multiple_of(k // 8 * PIECE + at * SLICE, SLICE), SLICE)
                ]
                place_s[k // 8, at] = jnp.where(here > 0, to + 1, 0)
                return count + jnp.where(here > 0, 1, 0)

            count = lax.fori_loop(0, 64, step, count, unroll=8)
    copy = pltpu.make_async_copy(place_s, flags_v, sem)
    copy.start()
    copy.wait()
    lane = lax.broadcasted_iota(jnp.int32, (SLICE, WIDTH), 1)
    sub = lax.broadcasted_iota(jnp.int32, (SLICE, WIDTH), 0)
    kept = flags_as_rows(c_pattern, lane)
    place = flags_v[...].astype(jnp.float32)
    place = jnp.where(lane < 32, jnp.concatenate([place, place], axis=0), jnp.float32(0.0))
    header = jnp.where(sub < 8, place, kept).astype(jnp.bfloat16)
    for ref in packed:
        ref[CAP * SLICE : (CAP + 1) * SLICE] = header


def pack_a(pieces, slots, c_pattern):
    out = jax.ShapeDtypeStruct((PACKED, WIDTH), jnp.bfloat16)
    return pl.pallas_call(
        pack_a_kernel,
        in_specs=[space(pltpu.SMEM)] * 2 + [space(pltpu.VMEM)],
        out_specs=[space(pltpu.VMEM)] * 2,
        out_shape=[out, out],
        scratch_shapes=[
            pltpu.VMEM((8, WIDTH), jnp.int32),
            pltpu.SMEM((8, WIDTH), jnp.int32),
            pltpu.SMEM((8, WIDTH), jnp.int32),
            pltpu.SemaphoreType.DMA,
        ],
    )(slots, c_pattern, pieces)


def pack_b_kernel(source, slots, *refs):
    pieces, pieces_a, packed = refs[:4], refs[4], refs[5]
    held, flags_v, flags_s, place_s, sem = refs[6:]
    flags_v[...] = jnp.zeros_like(flags_v)
    for n in range(4):
        row = pieces[n][32 * SLICE_B : PIECE_B].astype(jnp.float32).astype(jnp.int32)
        flags_v[pl.ds(source[n], 1)] = row[0:1]
    copy = pltpu.make_async_copy(flags_v, flags_s, sem)
    copy.start()
    for n in range(4):
        held[source[n]] = pieces[n][: 32 * SLICE_B]
    copy.wait()

    def step(n, count):
        m, at = n // 32, n % 32
        here = flags_s[m, at]
        to = jnp.minimum(count, CAP_B - 1)
        packed[pl.ds(pl.multiple_of(to * SLICE_B, SLICE_B), SLICE_B)] = held[
            m, pl.ds(pl.multiple_of(at * SLICE_B, SLICE_B), SLICE_B)
        ]
        place_s[m, at] = jnp.where(here > 0, to + 1, 0)
        return count + jnp.where(here > 0, 1, 0)

    lax.fori_loop(0, 128, step, jnp.int32(0), unroll=8)
    copy = pltpu.make_async_copy(place_s, flags_v, sem)
    copy.start()
    copy.wait()
    lane = lax.broadcasted_iota(jnp.int32, (SLICE, WIDTH), 1)
    place = flags_v[...].astype(jnp.float32)
    place = jnp.where((lane < 32) & (lax.broadcasted_iota(jnp.int32, (SLICE, WIDTH), 0) < 4), jnp.concatenate([place, place], axis=0), jnp.float32(0.0))
    in_a = jnp.zeros((SLICE, WIDTH), jnp.float32)
    sub = lax.broadcasted_iota(jnp.int32, (SLICE, WIDTH), 0)
    for m in range(8):
        row = pieces_a[PIECE * m + 32 * SLICE : PIECE * (m + 1)].astype(jnp.float32)
        in_a += row
        place = jnp.where((lane >= 32) & (lane < 64) & (sub == m), row, place)
    counts = []
    for pair in range(2):
        one, two = slots[2 * pair] * 8, slots[2 * pair + 1] * 8
        counted = ((lane >= one) & (lane < one + 8)) | ((lane >= two) & (lane < two + 8))
        counts.append(jnp.sum(jnp.where(counted & (sub == 0), in_a, jnp.float32(0.0))))
    over = jnp.where(jnp.maximum(counts[0], counts[1]) > CAP, jnp.float32(1.0), jnp.float32(0.0))
    packed[HEADER_B:PACKED_B] = jnp.where(sub < 8, place, over).astype(jnp.bfloat16)


def pack_b(pieces, source, pieces_a, slots):
    return pl.pallas_call(
        pack_b_kernel,
        in_specs=[space(pltpu.SMEM)] * 2 + [space(pltpu.VMEM)] * 5,
        out_specs=space(pltpu.VMEM),
        out_shape=jax.ShapeDtypeStruct((PACKED_B, WIDTH), jnp.bfloat16),
        scratch_shapes=[
            pltpu.VMEM((4, 32 * SLICE_B, WIDTH), jnp.bfloat16),
            pltpu.VMEM((8, WIDTH), jnp.int32),
            pltpu.SMEM((8, WIDTH), jnp.int32),
            pltpu.SMEM((8, WIDTH), jnp.int32),
            pltpu.SemaphoreType.DMA,
        ],
    )(source, slots, *pieces, pieces_a)


def product_kernel(source, slots, *refs):
    parts, panel, out, over = (refs[:4], refs[4:8]), refs[8], refs[9], refs[10]
    header_v, header_s, listed, rhs, lhs, total, sem = refs[11:]
    sub = lax.broadcasted_iota(jnp.int32, (SLICE, WIDTH), 0)
    lane = lax.broadcasted_iota(jnp.int32, (SLICE, WIDTH), 1)
    most_a, most_b = jnp.zeros((SLICE, WIDTH), jnp.float32), jnp.zeros((SLICE, 1), jnp.float32)
    for ring in range(4):
        count = jnp.zeros((SLICE, WIDTH), jnp.float32)
        for m in range(4):
            at = (m * 4 + ring) * PACKED_B + HEADER_B
            header = panel[at : at + SLICE].astype(jnp.float32)
            count += header
            most_a = jnp.maximum(most_a, header)
        count = jnp.where((lane >= 32) & (lane < 64) & (sub < 8), count, jnp.float32(0.0))
        most_b = jnp.maximum(most_b, jnp.sum(count, axis=1, keepdims=True))
    most_a = jnp.max(jnp.where(sub == 8, most_a, jnp.float32(0.0)))
    over[0] = ((most_a > 0) | (jnp.max(most_b) > CAP_B - 1)).astype(jnp.int32)
    for pair in range(2):
        at = CAP * SLICE
        header_v[pair * SLICE : (pair + 1) * SLICE] = parts[pair][0][at : at + SLICE].astype(jnp.float32).astype(jnp.int32)
    for n in range(4):
        at = n * PACKED_B + HEADER_B
        header_v[(2 + n) * SLICE : (3 + n) * SLICE] = panel[at : at + SLICE].astype(jnp.float32).astype(jnp.int32)
    copy = pltpu.make_async_copy(header_v, header_s, sem)
    copy.start()
    copy.wait()

    length = jnp.int32(0)
    chunks = []
    for pair in range(2):
        q0, q1 = slots[2 * pair], slots[2 * pair + 1]

        def step(k, length, pair=pair, q0=q0, q1=q1):
            first = header_s[pair * SLICE + k // 8, q0 * 8 + k % 8]
            second = header_s[pair * SLICE + k // 8, q1 * 8 + k % 8]
            listed[0, length] = k
            listed[1, length] = first
            listed[2, length] = second
            return length + jnp.where(first + second > 0, 1, 0)

        length = lax.fori_loop(0, 64, step, length, unroll=8)
        for i in range(CHUNK - 1):
            for n in range(3):
                listed[n, length + i] = 0
        length = (length + CHUNK - 1) // CHUNK * CHUNK
        chunks.append(length // CHUNK)
    total[...] = jnp.zeros_like(total)

    def multiply(chunk, carry, pair):
        for i in range(CHUNK):
            for slot in range(2):
                place = listed[1 + slot, chunk * CHUNK + i]
                at = jnp.maximum(place - 1, 0) * SLICE
                for dy in range(2):
                    for step in range(4):
                        value = parts[pair][step][pl.ds(pl.multiple_of(at + dy * PACKED, SLICE), SLICE)]
                        rows = pl.ds(pl.multiple_of(slot * WIDTH + source[dy * 4 + step] * SLICE, SLICE), SLICE)
                        lhs[rows, i * WIDTH : (i + 1) * WIDTH] = jnp.where(place > 0, value, jnp.zeros_like(value))
            k = listed[0, chunk * CHUNK + i]
            ring = k // 4 % 4
            for j in range(8):
                place = header_s[(2 + ring) * SLICE + k // 16, k % 4 * 8 + j]
                at = ring * PACKED_B + jnp.maximum(place - 1, 0) * SLICE_B
                for m in range(4):
                    value = panel[pl.ds(pl.multiple_of(at + m * 4 * PACKED_B, SLICE), SLICE_B)]
                    rhs[i * WIDTH + m * SLICE_B : i * WIDTH + (m + 1) * SLICE_B, j * WIDTH : (j + 1) * WIDTH] = jnp.where(
                        place > 0, value, jnp.zeros_like(value)
                    )
        for n in range(4):
            cols = slice(n * 256, (n + 1) * 256)
            total[pair, :, cols] += jnp.dot(lhs[...], rhs[:, cols], preferred_element_type=jnp.float32)
        return carry

    lax.fori_loop(0, chunks[0], functools.partial(multiply, pair=0), 0)
    lax.fori_loop(chunks[0], chunks[1], functools.partial(multiply, pair=1), 0)
    for slot in range(4):
        q = slots[slot]
        rows = slice(slot % 2 * WIDTH, (slot % 2 + 1) * WIDTH)
        for j in range(8):
            block = total[slot // 2, rows, j * WIDTH : (j + 1) * WIDTH]
            out[slot * WIDTH : (slot + 1) * WIDTH, j * WIDTH : (j + 1) * WIDTH] = jnp.where(
                header_s[slot // 2 * SLICE + 8, q * 8 + j] > 0, block, jnp.zeros_like(block)
            ).astype(jnp.bfloat16)


def packed_product(parts, panel, source, slots):
    return pl.pallas_call(
        product_kernel,
        in_specs=[space(pltpu.SMEM)] * 2 + [space(pltpu.VMEM)] * 9,
        out_specs=[space(pltpu.VMEM), space(pltpu.SMEM)],
        out_shape=[jax.ShapeDtypeStruct((512, 1024), jnp.bfloat16), jax.ShapeDtypeStruct((1,), jnp.int32)],
        scratch_shapes=[
            pltpu.VMEM((6 * SLICE, WIDTH), jnp.int32),
            pltpu.SMEM((6 * SLICE, WIDTH), jnp.int32),
            pltpu.SMEM((3, 2 * 64 + 2 * CHUNK), jnp.int32),
            pltpu.VMEM((CHUNK * WIDTH, 1024), jnp.bfloat16),
            pltpu.VMEM((2 * WIDTH, CHUNK * WIDTH), jnp.bfloat16),
            pltpu.VMEM((2, 2 * WIDTH, 1024), jnp.float32),
            pltpu.SemaphoreType.DMA,
        ],
        compiler_params=pltpu.CompilerParams(vmem_limit_bytes=24 * 2**20),
    )(source, slots, *parts, panel)


def dense_product(a, b, a_pattern, b_pattern, c_pattern, slots, slot_shift, source, row):
    value = masked(a, a_pattern)
    moved, kept = [], []
    for pair in range(2):
        rows = [lax.dynamic_slice_in_dim(value, slots[2 * pair + t] * WIDTH, WIDTH, 0) for t in range(2)]
        flags = [lax.dynamic_slice_in_dim(c_pattern, slots[2 * pair + t], 1, 0) for t in range(2)]
        moved.append(shifted(jnp.concatenate(rows, axis=0), ROW, 16, slot_shift[2 * pair]))
        kept.append(shifted(jnp.concatenate(flags, axis=0), ROW, 16, slot_shift[2 * pair]))
    value = jnp.concatenate(moved, axis=0)
    full = jnp.zeros((512, 8192), jnp.bfloat16)
    for t, offset in enumerate(OFFSETS):
        piece = from_offset(value, offset) if t else value
        full = lax.dynamic_update_slice(full, piece, (0, source[t] * 1024))
    own_b = masked(b, b_pattern)
    panel = jnp.zeros((8192, 1024), jnp.bfloat16)
    for by in range(16):
        piece = lax.ppermute(own_b, ROW, [((i + by) % 16, i) for i in range(16)]) if by else own_b
        panel = lax.dynamic_update_slice(panel, piece, ((row + by) % 16 * 512, 0))
    product = jnp.dot(full, panel, preferred_element_type=jnp.float32)
    mask = jnp.repeat(jnp.repeat(jnp.concatenate(kept, axis=0), WIDTH, axis=0), WIDTH, axis=1)
    return jnp.where(mask > 0, product, jnp.float32(0.0)).astype(jnp.bfloat16)


def local(a, b, a_pattern, b_pattern, c_pattern, owner_list):
    slot_shift = owner_list[:4] // 4 % 16
    slots = owner_list[:4] % 4
    yh, z = lax.axis_index("yh").astype(jnp.int32), lax.axis_index("z").astype(jnp.int32)
    row = lax.axis_index(ROW).astype(jnp.int32)
    ahead = jnp.stack([(yh + dy) % 2 * 4 + (z + dz) % 4 for dy, dz in OFFSETS])
    cut_a = cut(a, a_pattern, b_pattern)
    b_after, _ = lax.optimization_barrier((b, cut_a))
    pieces_a = lax.all_to_all(cut_a, COL, 0, 0, tiled=True)
    x = lax.axis_index("x").astype(jnp.int32)
    pieces_b = cut_b(b_after, b_pattern, jnp.stack([(x - n) % 4 for n in range(4)]))
    pieces_b = [from_ahead(piece, "x", n) if n else piece for n, piece in enumerate(pieces_b)]
    packed_b = pack_b(pieces_b, jnp.stack([(x + n) % 4 for n in range(4)]), pieces_a, slots)
    panel = lax.all_gather(packed_b, ROW, axis=0, tiled=True)
    first, second = pack_a(pieces_a, slots, c_pattern)
    parts = []
    for pair, packed in enumerate((first, second)):
        both = jnp.concatenate(shifted_both(packed, slot_shift[2 * pair]), axis=0)
        parts += [both] + [from_ahead(both, "z", step) for step in (1, 2, 3)]
    product, over = packed_product(parts, panel, ahead, slots)
    return lax.cond(
        over[0] > 0,
        lambda: dense_product(a, b, a_pattern, b_pattern, c_pattern, slots, slot_shift, ahead, row),
        lambda: product,
    )


def solution(mesh):
    fine = Mesh(mesh.devices.reshape(tuple(SIZES.values())), tuple(SIZES))
    return jax.shard_map(
        local,
        mesh=fine,
        in_specs=(P(ROW, COL),) * 5 + (P(),),
        out_specs=P(ROW, COL),
        check_vma=False,
    )
```

```python
import functools

import jax
import jax.numpy as jnp
from jax import lax
from jax.experimental import pallas as pl
from jax.experimental.pallas import tpu as pltpu
from jax.sharding import Mesh, PartitionSpec as P

SIZES = {"x": 4, "yl": 2, "core": 2, "yh": 2, "z": 4}
ROW = ("x", "yl", "core")
COL = ("yh", "z")
WIDTH = 128
SLICE = 16
CAP = 40
PIECE = 33 * SLICE
PACKED = (CAP + 1) * SLICE
SLICE_B = 32
CAP_B = 42
PIECE_B = 32 * SLICE_B + SLICE
HEADER_B = CAP_B * SLICE_B
PACKED_B = HEADER_B + SLICE
CHUNK = 4
OFFSETS = [(dy, dz) for dy in range(2) for dz in range(4)]


def space(kind):
    return pl.BlockSpec(memory_space=kind)


def from_ahead(value, axis, by):
    n = SIZES[axis]
    return lax.ppermute(value, axis, [((i + by) % n, i) for i in range(n)])


def from_offset(value, offset):
    return lax.ppermute(
        value,
        COL,
        [((y + offset[0]) % 2 * 4 + (z + offset[1]) % 4, y * 4 + z) for y in range(2) for z in range(4)],
    )


def shifted(value, axis, count, shift):
    def branch(by):
        perm = [((i + by) % count, i) for i in range(count)]
        return lambda v: lax.ppermute(v, axis, perm)

    return lax.switch(shift - 1, [branch(by) for by in range(1, count)], value)


def mask_kernel(pattern, ref, out):
    for i in range(4):
        for j in range(8):
            at = (slice(i * WIDTH, (i + 1) * WIDTH), slice(j * WIDTH, (j + 1) * WIDTH))
            block = ref[at]
            out[at] = jnp.where(pattern[i, j] > 0, block, jnp.zeros_like(block))


def masked(value, pattern):
    return pl.pallas_call(
        mask_kernel,
        in_specs=[space(pltpu.SMEM), space(pltpu.VMEM)],
        out_specs=space(pltpu.VMEM),
        out_shape=jax.ShapeDtypeStruct((512, 1024), jnp.bfloat16),
    )(pattern, value)


def flags_as_rows(flags, lane, first=0):
    row = jnp.zeros((SLICE, WIDTH), jnp.float32)
    for i in range(4):
        for j in range(8):
            row = jnp.where(lane == first + i * 8 + j, flags[i, j].astype(jnp.float32), row)
    return row


def cut_kernel(pattern, b_pattern, ref, out):
    lane = lax.broadcasted_iota(jnp.int32, (SLICE, WIDTH), 1)
    row = (flags_as_rows(pattern, lane) + flags_as_rows(b_pattern, lane, 32)).astype(jnp.bfloat16)
    for m in range(8):
        for i in range(4):
            rows = slice(i * WIDTH + m * SLICE, i * WIDTH + (m + 1) * SLICE)
            for j in range(8):
                at = PIECE * m + (i * 8 + j) * SLICE
                out[at : at + SLICE] = ref[rows, j * WIDTH : (j + 1) * WIDTH]
        out[PIECE * m + 32 * SLICE : PIECE * (m + 1)] = row


def cut(value, pattern, b_pattern):
    return pl.pallas_call(
        cut_kernel,
        in_specs=[space(pltpu.SMEM), space(pltpu.SMEM), space(pltpu.VMEM)],
        out_specs=space(pltpu.VMEM),
        out_shape=jax.ShapeDtypeStruct((8 * PIECE, WIDTH), jnp.bfloat16),
    )(pattern, b_pattern, value)


def cut_b_kernel(target, pattern, ref, *outs):
    lane = lax.broadcasted_iota(jnp.int32, (SLICE, WIDTH), 1)
    row = flags_as_rows(pattern, lane).astype(jnp.bfloat16)
    for n, out in enumerate(outs):
        for i in range(4):
            rows = pl.ds(pl.multiple_of(i * WIDTH + target[n] * SLICE_B, SLICE_B), SLICE_B)
            for j in range(8):
                at = (i * 8 + j) * SLICE_B
                out[at : at + SLICE_B] = ref[rows, j * WIDTH : (j + 1) * WIDTH]
        out[32 * SLICE_B : PIECE_B] = row


def cut_b(value, pattern, target):
    return pl.pallas_call(
        cut_b_kernel,
        in_specs=[space(pltpu.SMEM), space(pltpu.SMEM), space(pltpu.VMEM)],
        out_specs=[space(pltpu.VMEM)] * 4,
        out_shape=[jax.ShapeDtypeStruct((PIECE_B, WIDTH), jnp.bfloat16)] * 4,
    )(target, pattern, value)


def pack_a_kernel(slots, c_pattern, pieces, first, second, flags_v, flags_s, place_s, sem):
    packed = (first, second)
    for m in range(8):
        row = pieces[PIECE * m + 32 * SLICE : PIECE * (m + 1)].astype(jnp.float32).astype(jnp.int32)
        flags_v[m : m + 1] = row[0:1]
    copy = pltpu.make_async_copy(flags_v, flags_s, sem)
    copy.start()
    copy.wait()
    for pair in range(2):
        count = jnp.int32(0)
        for slot in range(2):
            q = slots[2 * pair + slot]

            def step(k, count, pair=pair, q=q):
                at = q * 8 + k % 8
                here = flags_s[k // 8, at]
                to = jnp.minimum(count, CAP)
                packed[pair][pl.ds(pl.multiple_of(to * SLICE, SLICE), SLICE)] = pieces[
                    pl.ds(pl.multiple_of(k // 8 * PIECE + at * SLICE, SLICE), SLICE)
                ]
                place_s[k // 8, at] = jnp.where(here > 0, to + 1, 0)
                return count + jnp.where(here > 0, 1, 0)

            count = lax.fori_loop(0, 64, step, count, unroll=8)
    copy = pltpu.make_async_copy(place_s, flags_v, sem)
    copy.start()
    copy.wait()
    lane = lax.broadcasted_iota(jnp.int32, (SLICE, WIDTH), 1)
    sub = lax.broadcasted_iota(jnp.int32, (SLICE, WIDTH), 0)
    kept = flags_as_rows(c_pattern, lane)
    place = flags_v[...].astype(jnp.float32)
    place = jnp.where(lane < 32, jnp.concatenate([place, place], axis=0), jnp.float32(0.0))
    header = jnp.where(sub < 8, place, kept).astype(jnp.bfloat16)
    for ref in packed:
        ref[CAP * SLICE : (CAP + 1) * SLICE] = header


def pack_a(pieces, slots, c_pattern):
    out = jax.ShapeDtypeStruct((PACKED, WIDTH), jnp.bfloat16)
    return pl.pallas_call(
        pack_a_kernel,
        in_specs=[space(pltpu.SMEM)] * 2 + [space(pltpu.VMEM)],
        out_specs=[space(pltpu.VMEM)] * 2,
        out_shape=[out, out],
        scratch_shapes=[
            pltpu.VMEM((8, WIDTH), jnp.int32),
            pltpu.SMEM((8, WIDTH), jnp.int32),
            pltpu.SMEM((8, WIDTH), jnp.int32),
            pltpu.SemaphoreType.DMA,
        ],
    )(slots, c_pattern, pieces)


def pack_b_kernel(source, slots, *refs):
    pieces, pieces_a, packed = refs[:4], refs[4], refs[5]
    held, flags_v, flags_s, place_s, sem = refs[6:]
    flags_v[...] = jnp.zeros_like(flags_v)
    for n in range(4):
        row = pieces[n][32 * SLICE_B : PIECE_B].astype(jnp.float32).astype(jnp.int32)
        flags_v[pl.ds(source[n], 1)] = row[0:1]
    copy = pltpu.make_async_copy(flags_v, flags_s, sem)
    copy.start()
    for n in range(4):
        held[source[n]] = pieces[n][: 32 * SLICE_B]
    copy.wait()

    def step(n, count):
        m, at = n // 32, n % 32
        here = flags_s[m, at]
        to = jnp.minimum(count, CAP_B - 1)
        packed[pl.ds(pl.multiple_of(to * SLICE_B, SLICE_B), SLICE_B)] = held[
            m, pl.ds(pl.multiple_of(at * SLICE_B, SLICE_B), SLICE_B)
        ]
        place_s[m, at] = jnp.where(here > 0, to + 1, 0)
        return count + jnp.where(here > 0, 1, 0)

    lax.fori_loop(0, 128, step, jnp.int32(0), unroll=8)
    copy = pltpu.make_async_copy(place_s, flags_v, sem)
    copy.start()
    copy.wait()
    lane = lax.broadcasted_iota(jnp.int32, (SLICE, WIDTH), 1)
    place = flags_v[...].astype(jnp.float32)
    place = jnp.where((lane < 32) & (lax.broadcasted_iota(jnp.int32, (SLICE, WIDTH), 0) < 4), jnp.concatenate([place, place], axis=0), jnp.float32(0.0))
    in_a = jnp.zeros((SLICE, WIDTH), jnp.float32)
    sub = lax.broadcasted_iota(jnp.int32, (SLICE, WIDTH), 0)
    for m in range(8):
        row = pieces_a[PIECE * m + 32 * SLICE : PIECE * (m + 1)].astype(jnp.float32)
        in_a += row
        place = jnp.where((lane >= 32) & (lane < 64) & (sub == m), row, place)
    counts = []
    for pair in range(2):
        one, two = slots[2 * pair] * 8, slots[2 * pair + 1] * 8
        counted = ((lane >= one) & (lane < one + 8)) | ((lane >= two) & (lane < two + 8))
        counts.append(jnp.sum(jnp.where(counted & (sub == 0), in_a, jnp.float32(0.0))))
    over = jnp.where(jnp.maximum(counts[0], counts[1]) > CAP, jnp.float32(1.0), jnp.float32(0.0))
    packed[HEADER_B:PACKED_B] = jnp.where(sub < 8, place, over).astype(jnp.bfloat16)


def pack_b(pieces, source, pieces_a, slots):
    return pl.pallas_call(
        pack_b_kernel,
        in_specs=[space(pltpu.SMEM)] * 2 + [space(pltpu.VMEM)] * 5,
        out_specs=space(pltpu.VMEM),
        out_shape=jax.ShapeDtypeStruct((PACKED_B, WIDTH), jnp.bfloat16),
        scratch_shapes=[
            pltpu.VMEM((4, 32 * SLICE_B, WIDTH), jnp.bfloat16),
            pltpu.VMEM((8, WIDTH), jnp.int32),
            pltpu.SMEM((8, WIDTH), jnp.int32),
            pltpu.SMEM((8, WIDTH), jnp.int32),
            pltpu.SemaphoreType.DMA,
        ],
    )(source, slots, *pieces, pieces_a)


def product_kernel(source, slots, *refs):
    parts, panel, out, over = (refs[:4], refs[4:8]), refs[8], refs[9], refs[10]
    header_v, header_s, listed, rhs, lhs, total, sem = refs[11:]
    sub = lax.broadcasted_iota(jnp.int32, (SLICE, WIDTH), 0)
    lane = lax.broadcasted_iota(jnp.int32, (SLICE, WIDTH), 1)
    most_a, most_b = jnp.zeros((SLICE, WIDTH), jnp.float32), jnp.zeros((SLICE, 1), jnp.float32)
    for ring in range(4):
        count = jnp.zeros((SLICE, WIDTH), jnp.float32)
        for m in range(4):
            at = (m * 4 + ring) * PACKED_B + HEADER_B
            header = panel[at : at + SLICE].astype(jnp.float32)
            count += header
            most_a = jnp.maximum(most_a, header)
        count = jnp.where((lane >= 32) & (lane < 64) & (sub < 8), count, jnp.float32(0.0))
        most_b = jnp.maximum(most_b, jnp.sum(count, axis=1, keepdims=True))
    most_a = jnp.max(jnp.where(sub == 8, most_a, jnp.float32(0.0)))
    over[0] = ((most_a > 0) | (jnp.max(most_b) > CAP_B - 1)).astype(jnp.int32)
    for pair in range(2):
        at = CAP * SLICE
        header_v[pair * SLICE : (pair + 1) * SLICE] = parts[pair][0][at : at + SLICE].astype(jnp.float32).astype(jnp.int32)
    for n in range(4):
        at = n * PACKED_B + HEADER_B
        header_v[(2 + n) * SLICE : (3 + n) * SLICE] = panel[at : at + SLICE].astype(jnp.float32).astype(jnp.int32)
    copy = pltpu.make_async_copy(header_v, header_s, sem)
    copy.start()
    copy.wait()

    length = jnp.int32(0)
    chunks = []
    for pair in range(2):
        q0, q1 = slots[2 * pair], slots[2 * pair + 1]

        def step(k, length, pair=pair, q0=q0, q1=q1):
            first = header_s[pair * SLICE + k // 8, q0 * 8 + k % 8]
            second = header_s[pair * SLICE + k // 8, q1 * 8 + k % 8]
            listed[0, length] = k
            listed[1, length] = first
            listed[2, length] = second
            return length + jnp.where(first + second > 0, 1, 0)

        length = lax.fori_loop(0, 64, step, length, unroll=8)
        for i in range(CHUNK - 1):
            for n in range(3):
                listed[n, length + i] = 0
        length = (length + CHUNK - 1) // CHUNK * CHUNK
        chunks.append(length // CHUNK)
    total[...] = jnp.zeros_like(total)

    def multiply(chunk, carry, pair):
        for i in range(CHUNK):
            for slot in range(2):
                place = listed[1 + slot, chunk * CHUNK + i]
                at = jnp.maximum(place - 1, 0) * SLICE
                for dy in range(2):
                    for step in range(4):
                        value = parts[pair][step][pl.ds(pl.multiple_of(at + dy * PACKED, SLICE), SLICE)]
                        rows = pl.ds(pl.multiple_of(slot * WIDTH + source[dy * 4 + step] * SLICE, SLICE), SLICE)
                        lhs[rows, i * WIDTH : (i + 1) * WIDTH] = jnp.where(place > 0, value, jnp.zeros_like(value))
            k = listed[0, chunk * CHUNK + i]
            ring = k // 4 % 4
            for j in range(8):
                place = header_s[(2 + ring) * SLICE + k // 16, k % 4 * 8 + j]
                at = ring * PACKED_B + jnp.maximum(place - 1, 0) * SLICE_B
                for m in range(4):
                    value = panel[pl.ds(pl.multiple_of(at + m * 4 * PACKED_B, SLICE), SLICE_B)]
                    rhs[i * WIDTH + m * SLICE_B : i * WIDTH + (m + 1) * SLICE_B, j * WIDTH : (j + 1) * WIDTH] = jnp.where(
                        place > 0, value, jnp.zeros_like(value)
                    )
        for n in range(4):
            cols = slice(n * 256, (n + 1) * 256)
            total[pair, :, cols] += jnp.dot(lhs[...], rhs[:, cols], preferred_element_type=jnp.float32)
        return carry

    lax.fori_loop(0, chunks[0], functools.partial(multiply, pair=0), 0)
    lax.fori_loop(chunks[0], chunks[1], functools.partial(multiply, pair=1), 0)
    for slot in range(4):
        q = slots[slot]
        rows = slice(slot % 2 * WIDTH, (slot % 2 + 1) * WIDTH)
        for j in range(8):
            block = total[slot // 2, rows, j * WIDTH : (j + 1) * WIDTH]
            out[slot * WIDTH : (slot + 1) * WIDTH, j * WIDTH : (j + 1) * WIDTH] = jnp.where(
                header_s[slot // 2 * SLICE + 8, q * 8 + j] > 0, block, jnp.zeros_like(block)
            ).astype(jnp.bfloat16)


def packed_product(parts, panel, source, slots):
    return pl.pallas_call(
        product_kernel,
        in_specs=[space(pltpu.SMEM)] * 2 + [space(pltpu.VMEM)] * 9,
        out_specs=[space(pltpu.VMEM), space(pltpu.SMEM)],
        out_shape=[jax.ShapeDtypeStruct((512, 1024), jnp.bfloat16), jax.ShapeDtypeStruct((1,), jnp.int32)],
        scratch_shapes=[
            pltpu.VMEM((6 * SLICE, WIDTH), jnp.int32),
            pltpu.SMEM((6 * SLICE, WIDTH), jnp.int32),
            pltpu.SMEM((3, 2 * 64 + 2 * CHUNK), jnp.int32),
            pltpu.VMEM((CHUNK * WIDTH, 1024), jnp.bfloat16),
            pltpu.VMEM((2 * WIDTH, CHUNK * WIDTH), jnp.bfloat16),
            pltpu.VMEM((2, 2 * WIDTH, 1024), jnp.float32),
            pltpu.SemaphoreType.DMA,
        ],
        compiler_params=pltpu.CompilerParams(vmem_limit_bytes=24 * 2**20),
    )(source, slots, *parts, panel)


def dense_product(a, b, a_pattern, b_pattern, c_pattern, slots, slot_shift, source, row):
    value = masked(a, a_pattern)
    moved, kept = [], []
    for pair in range(2):
        rows = [lax.dynamic_slice_in_dim(value, slots[2 * pair + t] * WIDTH, WIDTH, 0) for t in range(2)]
        flags = [lax.dynamic_slice_in_dim(c_pattern, slots[2 * pair + t], 1, 0) for t in range(2)]
        moved.append(shifted(jnp.concatenate(rows, axis=0), ROW, 16, slot_shift[2 * pair]))
        kept.append(shifted(jnp.concatenate(flags, axis=0), ROW, 16, slot_shift[2 * pair]))
    value = jnp.concatenate(moved, axis=0)
    full = jnp.zeros((512, 8192), jnp.bfloat16)
    for t, offset in enumerate(OFFSETS):
        piece = from_offset(value, offset) if t else value
        full = lax.dynamic_update_slice(full, piece, (0, source[t] * 1024))
    own_b = masked(b, b_pattern)
    panel = jnp.zeros((8192, 1024), jnp.bfloat16)
    for by in range(16):
        piece = lax.ppermute(own_b, ROW, [((i + by) % 16, i) for i in range(16)]) if by else own_b
        panel = lax.dynamic_update_slice(panel, piece, ((row + by) % 16 * 512, 0))
    product = jnp.dot(full, panel, preferred_element_type=jnp.float32)
    mask = jnp.repeat(jnp.repeat(jnp.concatenate(kept, axis=0), WIDTH, axis=0), WIDTH, axis=1)
    return jnp.where(mask > 0, product, jnp.float32(0.0)).astype(jnp.bfloat16)


def local(a, b, a_pattern, b_pattern, c_pattern, owner_list):
    slot_shift = owner_list[:4] // 4 % 16
    slots = owner_list[:4] % 4
    yh, z = lax.axis_index("yh").astype(jnp.int32), lax.axis_index("z").astype(jnp.int32)
    row = lax.axis_index(ROW).astype(jnp.int32)
    ahead = jnp.stack([(yh + dy) % 2 * 4 + (z + dz) % 4 for dy, dz in OFFSETS])
    cut_a = cut(a, a_pattern, b_pattern)
    b_after, _ = lax.optimization_barrier((b, cut_a))
    pieces_a = lax.all_to_all(cut_a, COL, 0, 0, tiled=True)
    x = lax.axis_index("x").astype(jnp.int32)
    pieces_b = cut_b(b_after, b_pattern, jnp.stack([(x - n) % 4 for n in range(4)]))
    pieces_b = [from_ahead(piece, "x", n) if n else piece for n, piece in enumerate(pieces_b)]
    packed_b = pack_b(pieces_b, jnp.stack([(x + n) % 4 for n in range(4)]), pieces_a, slots)
    panel = lax.all_gather(packed_b, ROW, axis=0, tiled=True)
    first, second = pack_a(pieces_a, slots, c_pattern)
    parts = []
    for pair, packed in enumerate((first, second)):
        moved = shifted(packed, ROW, 16, slot_shift[2 * pair])
        both = jnp.concatenate([moved, from_ahead(moved, "yh", 1)], axis=0)
        parts += [both] + [from_ahead(both, "z", step) for step in (1, 2, 3)]
    product, over = packed_product(parts, panel, ahead, slots)
    return lax.cond(
        over[0] > 0,
        lambda: dense_product(a, b, a_pattern, b_pattern, c_pattern, slots, slot_shift, ahead, row),
        lambda: product,
    )


def solution(mesh):
    fine = Mesh(mesh.devices.reshape(tuple(SIZES.values())), tuple(SIZES))
    return jax.shard_map(
        local,
        mesh=fine,
        in_specs=(P(ROW, COL),) * 5 + (P(),),
        out_specs=P(ROW, COL),
        check_vma=False,
    )
```

```python
import functools

import jax
import jax.numpy as jnp
from jax import lax
from jax.experimental import pallas as pl
from jax.experimental.pallas import tpu as pltpu
from jax.sharding import Mesh, PartitionSpec as P

SIZES = {"x": 4, "yl": 2, "core": 2, "yh": 2, "z": 4}
ROW = ("x", "yl", "core")
COL = ("yh", "z")
WIDTH = 128
SLICE = 16
CAP = 40
PIECE = 33 * SLICE
PACKED = (CAP + 1) * SLICE
SLICE_B = 32
CAP_B = 42
PIECE_B = 32 * SLICE_B + SLICE
HEADER_B = CAP_B * SLICE_B
PACKED_B = HEADER_B + SLICE
CHUNK = 4
OFFSETS = [(dy, dz) for dy in range(2) for dz in range(4)]


def space(kind):
    return pl.BlockSpec(memory_space=kind)


def from_ahead(value, axis, by):
    n = SIZES[axis]
    return lax.ppermute(value, axis, [((i + by) % n, i) for i in range(n)])


def from_offset(value, offset):
    return lax.ppermute(
        value,
        COL,
        [((y + offset[0]) % 2 * 4 + (z + offset[1]) % 4, y * 4 + z) for y in range(2) for z in range(4)],
    )


def shifted(value, axis, count, shift):
    def branch(by):
        perm = [((i + by) % count, i) for i in range(count)]
        return lambda v: lax.ppermute(v, axis, perm)

    return lax.switch(shift - 1, [branch(by) for by in range(1, count)], value)


def mask_kernel(pattern, ref, out):
    for i in range(4):
        for j in range(8):
            at = (slice(i * WIDTH, (i + 1) * WIDTH), slice(j * WIDTH, (j + 1) * WIDTH))
            block = ref[at]
            out[at] = jnp.where(pattern[i, j] > 0, block, jnp.zeros_like(block))


def masked(value, pattern):
    return pl.pallas_call(
        mask_kernel,
        in_specs=[space(pltpu.SMEM), space(pltpu.VMEM)],
        out_specs=space(pltpu.VMEM),
        out_shape=jax.ShapeDtypeStruct((512, 1024), jnp.bfloat16),
    )(pattern, value)


def flags_as_rows(flags, lane, first=0):
    row = jnp.zeros((SLICE, WIDTH), jnp.float32)
    for i in range(4):
        for j in range(8):
            row = jnp.where(lane == first + i * 8 + j, flags[i, j].astype(jnp.float32), row)
    return row


def cut_kernel(pattern, b_pattern, ref, out):
    lane = lax.broadcasted_iota(jnp.int32, (SLICE, WIDTH), 1)
    row = (flags_as_rows(pattern, lane) + flags_as_rows(b_pattern, lane, 32)).astype(jnp.bfloat16)
    for m in range(8):
        for i in range(4):
            rows = slice(i * WIDTH + m * SLICE, i * WIDTH + (m + 1) * SLICE)
            for j in range(8):
                at = PIECE * m + (i * 8 + j) * SLICE
                out[at : at + SLICE] = ref[rows, j * WIDTH : (j + 1) * WIDTH]
        out[PIECE * m + 32 * SLICE : PIECE * (m + 1)] = row


def cut(value, pattern, b_pattern):
    return pl.pallas_call(
        cut_kernel,
        in_specs=[space(pltpu.SMEM), space(pltpu.SMEM), space(pltpu.VMEM)],
        out_specs=space(pltpu.VMEM),
        out_shape=jax.ShapeDtypeStruct((8 * PIECE, WIDTH), jnp.bfloat16),
    )(pattern, b_pattern, value)


def cut_b_kernel(target, pattern, ref, *outs):
    lane = lax.broadcasted_iota(jnp.int32, (SLICE, WIDTH), 1)
    row = flags_as_rows(pattern, lane).astype(jnp.bfloat16)
    for n, out in enumerate(outs):
        for i in range(4):
            rows = pl.ds(pl.multiple_of(i * WIDTH + target[n] * SLICE_B, SLICE_B), SLICE_B)
            for j in range(8):
                at = (i * 8 + j) * SLICE_B
                out[at : at + SLICE_B] = ref[rows, j * WIDTH : (j + 1) * WIDTH]
        out[32 * SLICE_B : PIECE_B] = row


def cut_b(value, pattern, target):
    return pl.pallas_call(
        cut_b_kernel,
        in_specs=[space(pltpu.SMEM), space(pltpu.SMEM), space(pltpu.VMEM)],
        out_specs=[space(pltpu.VMEM)] * 4,
        out_shape=[jax.ShapeDtypeStruct((PIECE_B, WIDTH), jnp.bfloat16)] * 4,
    )(target, pattern, value)


def pack_a_kernel(slots, c_pattern, pieces, first, second, flags_v, flags_s, place_s, sem):
    packed = (first, second)
    for m in range(8):
        row = pieces[PIECE * m + 32 * SLICE : PIECE * (m + 1)].astype(jnp.float32).astype(jnp.int32)
        flags_v[m : m + 1] = row[0:1]
    copy = pltpu.make_async_copy(flags_v, flags_s, sem)
    copy.start()
    copy.wait()
    for pair in range(2):
        count = jnp.int32(0)
        for slot in range(2):
            q = slots[2 * pair + slot]

            def step(k, count, pair=pair, q=q):
                at = q * 8 + k % 8
                here = flags_s[k // 8, at]
                to = jnp.minimum(count, CAP)
                packed[pair][pl.ds(pl.multiple_of(to * SLICE, SLICE), SLICE)] = pieces[
                    pl.ds(pl.multiple_of(k // 8 * PIECE + at * SLICE, SLICE), SLICE)
                ]
                place_s[k // 8, at] = jnp.where(here > 0, to + 1, 0)
                return count + jnp.where(here > 0, 1, 0)

            count = lax.fori_loop(0, 64, step, count, unroll=8)
    copy = pltpu.make_async_copy(place_s, flags_v, sem)
    copy.start()
    copy.wait()
    lane = lax.broadcasted_iota(jnp.int32, (SLICE, WIDTH), 1)
    sub = lax.broadcasted_iota(jnp.int32, (SLICE, WIDTH), 0)
    kept = flags_as_rows(c_pattern, lane)
    place = flags_v[...].astype(jnp.float32)
    place = jnp.where(lane < 32, jnp.concatenate([place, place], axis=0), jnp.float32(0.0))
    header = jnp.where(sub < 8, place, kept).astype(jnp.bfloat16)
    for ref in packed:
        ref[CAP * SLICE : (CAP + 1) * SLICE] = header


def pack_a(pieces, slots, c_pattern):
    out = jax.ShapeDtypeStruct((PACKED, WIDTH), jnp.bfloat16)
    return pl.pallas_call(
        pack_a_kernel,
        in_specs=[space(pltpu.SMEM)] * 2 + [space(pltpu.VMEM)],
        out_specs=[space(pltpu.VMEM)] * 2,
        out_shape=[out, out],
        scratch_shapes=[
            pltpu.VMEM((8, WIDTH), jnp.int32),
            pltpu.SMEM((8, WIDTH), jnp.int32),
            pltpu.SMEM((8, WIDTH), jnp.int32),
            pltpu.SemaphoreType.DMA,
        ],
    )(slots, c_pattern, pieces)


def pack_b_kernel(source, slots, *refs):
    pieces, pieces_a, packed = refs[:4], refs[4], refs[5]
    held, flags_v, flags_s, place_s, sem = refs[6:]
    flags_v[...] = jnp.zeros_like(flags_v)
    for n in range(4):
        row = pieces[n][32 * SLICE_B : PIECE_B].astype(jnp.float32).astype(jnp.int32)
        flags_v[pl.ds(source[n], 1)] = row[0:1]
    copy = pltpu.make_async_copy(flags_v, flags_s, sem)
    copy.start()
    for n in range(4):
        held[source[n]] = pieces[n][: 32 * SLICE_B]
    copy.wait()

    def step(n, count):
        m, at = n // 32, n % 32
        here = flags_s[m, at]
        to = jnp.minimum(count, CAP_B - 1)
        packed[pl.ds(pl.multiple_of(to * SLICE_B, SLICE_B), SLICE_B)] = held[
            m, pl.ds(pl.multiple_of(at * SLICE_B, SLICE_B), SLICE_B)
        ]
        place_s[m, at] = jnp.where(here > 0, to + 1, 0)
        return count + jnp.where(here > 0, 1, 0)

    lax.fori_loop(0, 128, step, jnp.int32(0), unroll=8)
    copy = pltpu.make_async_copy(place_s, flags_v, sem)
    copy.start()
    copy.wait()
    lane = lax.broadcasted_iota(jnp.int32, (SLICE, WIDTH), 1)
    place = flags_v[...].astype(jnp.float32)
    place = jnp.where((lane < 32) & (lax.broadcasted_iota(jnp.int32, (SLICE, WIDTH), 0) < 4), jnp.concatenate([place, place], axis=0), jnp.float32(0.0))
    in_a = jnp.zeros((SLICE, WIDTH), jnp.float32)
    sub = lax.broadcasted_iota(jnp.int32, (SLICE, WIDTH), 0)
    for m in range(8):
        row = pieces_a[PIECE * m + 32 * SLICE : PIECE * (m + 1)].astype(jnp.float32)
        in_a += row
        place = jnp.where((lane >= 32) & (lane < 64) & (sub == m), row, place)
    counts = []
    for pair in range(2):
        one, two = slots[2 * pair] * 8, slots[2 * pair + 1] * 8
        counted = ((lane >= one) & (lane < one + 8)) | ((lane >= two) & (lane < two + 8))
        counts.append(jnp.sum(jnp.where(counted & (sub == 0), in_a, jnp.float32(0.0))))
    over = jnp.where(jnp.maximum(counts[0], counts[1]) > CAP, jnp.float32(1.0), jnp.float32(0.0))
    packed[HEADER_B:PACKED_B] = jnp.where(sub < 8, place, over).astype(jnp.bfloat16)


def pack_b(pieces, source, pieces_a, slots):
    return pl.pallas_call(
        pack_b_kernel,
        in_specs=[space(pltpu.SMEM)] * 2 + [space(pltpu.VMEM)] * 5,
        out_specs=space(pltpu.VMEM),
        out_shape=jax.ShapeDtypeStruct((PACKED_B, WIDTH), jnp.bfloat16),
        scratch_shapes=[
            pltpu.VMEM((4, 32 * SLICE_B, WIDTH), jnp.bfloat16),
            pltpu.VMEM((8, WIDTH), jnp.int32),
            pltpu.SMEM((8, WIDTH), jnp.int32),
            pltpu.SMEM((8, WIDTH), jnp.int32),
            pltpu.SemaphoreType.DMA,
        ],
    )(source, slots, *pieces, pieces_a)


def over_kernel(headers, over):
    sub = lax.broadcasted_iota(jnp.int32, (SLICE, WIDTH), 0)
    lane = lax.broadcasted_iota(jnp.int32, (SLICE, WIDTH), 1)
    most_a, most_b = jnp.zeros((SLICE, WIDTH), jnp.float32), jnp.zeros((SLICE, 1), jnp.float32)
    for ring in range(4):
        count = jnp.zeros((SLICE, WIDTH), jnp.float32)
        for m in range(4):
            header = headers[m * 4 + ring].astype(jnp.float32)
            count += header
            most_a = jnp.maximum(most_a, header)
        count = jnp.where((lane >= 32) & (lane < 64) & (sub < 8), count, jnp.float32(0.0))
        most_b = jnp.maximum(most_b, jnp.sum(count, axis=1, keepdims=True))
    most_a = jnp.max(jnp.where(sub == 8, most_a, jnp.float32(0.0)))
    over[0] = ((most_a > 0) | (jnp.max(most_b) > CAP_B - 1)).astype(jnp.int32)


def over_capacity(headers):
    return pl.pallas_call(
        over_kernel,
        in_specs=[space(pltpu.VMEM)],
        out_specs=space(pltpu.SMEM),
        out_shape=jax.ShapeDtypeStruct((1,), jnp.int32),
    )(headers)


def product_kernel(source, slots, *refs):
    parts, panel, out = (refs[:4], refs[4:8]), refs[8], refs[9]
    header_v, header_s, listed, rhs, lhs, total, sem = refs[10:]
    for pair in range(2):
        at = CAP * SLICE
        header_v[pair * SLICE : (pair + 1) * SLICE] = parts[pair][0][at : at + SLICE].astype(jnp.float32).astype(jnp.int32)
    for n in range(4):
        at = n * PACKED_B + HEADER_B
        header_v[(2 + n) * SLICE : (3 + n) * SLICE] = panel[at : at + SLICE].astype(jnp.float32).astype(jnp.int32)
    copy = pltpu.make_async_copy(header_v, header_s, sem)
    copy.start()
    copy.wait()

    length = jnp.int32(0)
    chunks = []
    for pair in range(2):
        q0, q1 = slots[2 * pair], slots[2 * pair + 1]

        def step(k, length, pair=pair, q0=q0, q1=q1):
            first = header_s[pair * SLICE + k // 8, q0 * 8 + k % 8]
            second = header_s[pair * SLICE + k // 8, q1 * 8 + k % 8]
            listed[0, length] = k
            listed[1, length] = first
            listed[2, length] = second
            return length + jnp.where(first + second > 0, 1, 0)

        length = lax.fori_loop(0, 64, step, length, unroll=8)
        for i in range(CHUNK - 1):
            for n in range(3):
                listed[n, length + i] = 0
        length = (length + CHUNK - 1) // CHUNK * CHUNK
        chunks.append(length // CHUNK)
    total[...] = jnp.zeros_like(total)

    def multiply(chunk, carry, pair):
        for i in range(CHUNK):
            for slot in range(2):
                place = listed[1 + slot, chunk * CHUNK + i]
                at = jnp.maximum(place - 1, 0) * SLICE
                for dy in range(2):
                    for step in range(4):
                        value = parts[pair][step][pl.ds(pl.multiple_of(at + dy * PACKED, SLICE), SLICE)]
                        rows = pl.ds(pl.multiple_of(slot * WIDTH + source[dy * 4 + step] * SLICE, SLICE), SLICE)
                        lhs[rows, i * WIDTH : (i + 1) * WIDTH] = jnp.where(place > 0, value, jnp.zeros_like(value))
            k = listed[0, chunk * CHUNK + i]
            ring = k // 4 % 4
            for j in range(8):
                place = header_s[(2 + ring) * SLICE + k // 16, k % 4 * 8 + j]
                at = ring * PACKED_B + jnp.maximum(place - 1, 0) * SLICE_B
                for m in range(4):
                    value = panel[pl.ds(pl.multiple_of(at + m * 4 * PACKED_B, SLICE), SLICE_B)]
                    rhs[i * WIDTH + m * SLICE_B : i * WIDTH + (m + 1) * SLICE_B, j * WIDTH : (j + 1) * WIDTH] = jnp.where(
                        place > 0, value, jnp.zeros_like(value)
                    )
        for n in range(4):
            cols = slice(n * 256, (n + 1) * 256)
            total[pair, :, cols] += jnp.dot(lhs[...], rhs[:, cols], preferred_element_type=jnp.float32)
        return carry

    lax.fori_loop(0, chunks[0], functools.partial(multiply, pair=0), 0)
    lax.fori_loop(chunks[0], chunks[1], functools.partial(multiply, pair=1), 0)
    for slot in range(4):
        q = slots[slot]
        rows = slice(slot % 2 * WIDTH, (slot % 2 + 1) * WIDTH)
        for j in range(8):
            block = total[slot // 2, rows, j * WIDTH : (j + 1) * WIDTH]
            out[slot * WIDTH : (slot + 1) * WIDTH, j * WIDTH : (j + 1) * WIDTH] = jnp.where(
                header_s[slot // 2 * SLICE + 8, q * 8 + j] > 0, block, jnp.zeros_like(block)
            ).astype(jnp.bfloat16)


def packed_product(parts, panel, source, slots):
    return pl.pallas_call(
        product_kernel,
        in_specs=[space(pltpu.SMEM)] * 2 + [space(pltpu.VMEM)] * 9,
        out_specs=space(pltpu.VMEM),
        out_shape=jax.ShapeDtypeStruct((512, 1024), jnp.bfloat16),
        scratch_shapes=[
            pltpu.VMEM((6 * SLICE, WIDTH), jnp.int32),
            pltpu.SMEM((6 * SLICE, WIDTH), jnp.int32),
            pltpu.SMEM((3, 2 * 64 + 2 * CHUNK), jnp.int32),
            pltpu.VMEM((CHUNK * WIDTH, 1024), jnp.bfloat16),
            pltpu.VMEM((2 * WIDTH, CHUNK * WIDTH), jnp.bfloat16),
            pltpu.VMEM((2, 2 * WIDTH, 1024), jnp.float32),
            pltpu.SemaphoreType.DMA,
        ],
        compiler_params=pltpu.CompilerParams(vmem_limit_bytes=24 * 2**20),
    )(source, slots, *parts, panel)


def dense_product(a, b, a_pattern, b_pattern, c_pattern, slots, slot_shift, source, row):
    value = masked(a, a_pattern)
    moved, kept = [], []
    for pair in range(2):
        rows = [lax.dynamic_slice_in_dim(value, slots[2 * pair + t] * WIDTH, WIDTH, 0) for t in range(2)]
        flags = [lax.dynamic_slice_in_dim(c_pattern, slots[2 * pair + t], 1, 0) for t in range(2)]
        moved.append(shifted(jnp.concatenate(rows, axis=0), ROW, 16, slot_shift[2 * pair]))
        kept.append(shifted(jnp.concatenate(flags, axis=0), ROW, 16, slot_shift[2 * pair]))
    value = jnp.concatenate(moved, axis=0)
    full = jnp.zeros((512, 8192), jnp.bfloat16)
    for t, offset in enumerate(OFFSETS):
        piece = from_offset(value, offset) if t else value
        full = lax.dynamic_update_slice(full, piece, (0, source[t] * 1024))
    own_b = masked(b, b_pattern)
    panel = jnp.zeros((8192, 1024), jnp.bfloat16)
    for by in range(16):
        piece = lax.ppermute(own_b, ROW, [((i + by) % 16, i) for i in range(16)]) if by else own_b
        panel = lax.dynamic_update_slice(panel, piece, ((row + by) % 16 * 512, 0))
    product = jnp.dot(full, panel, preferred_element_type=jnp.float32)
    mask = jnp.repeat(jnp.repeat(jnp.concatenate(kept, axis=0), WIDTH, axis=0), WIDTH, axis=1)
    return jnp.where(mask > 0, product, jnp.float32(0.0)).astype(jnp.bfloat16)


def local(a, b, a_pattern, b_pattern, c_pattern, owner_list):
    slot_shift = owner_list[:4] // 4 % 16
    slots = owner_list[:4] % 4
    yh, z = lax.axis_index("yh").astype(jnp.int32), lax.axis_index("z").astype(jnp.int32)
    row = lax.axis_index(ROW).astype(jnp.int32)
    ahead = jnp.stack([(yh + dy) % 2 * 4 + (z + dz) % 4 for dy, dz in OFFSETS])
    cut_a = cut(a, a_pattern, b_pattern)
    b_after, _ = lax.optimization_barrier((b, cut_a))
    pieces_a = lax.all_to_all(cut_a, COL, 0, 0, tiled=True)
    x = lax.axis_index("x").astype(jnp.int32)
    pieces_b = cut_b(b_after, b_pattern, jnp.stack([(x - n) % 4 for n in range(4)]))
    pieces_b = [from_ahead(piece, "x", n) if n else piece for n, piece in enumerate(pieces_b)]
    packed_b = pack_b(pieces_b, jnp.stack([(x + n) % 4 for n in range(4)]), pieces_a, slots)
    panel = lax.all_gather(packed_b, ROW, axis=0, tiled=True)
    first, second = pack_a(pieces_a, slots, c_pattern)
    parts = []
    for pair, packed in enumerate((first, second)):
        moved = shifted(packed, ROW, 16, slot_shift[2 * pair])
        both = jnp.concatenate([moved, from_ahead(moved, "yh", 1)], axis=0)
        parts += [both] + [from_ahead(both, "z", step) for step in (1, 2, 3)]
    over = over_capacity(panel.reshape(16, PACKED_B, WIDTH)[:, HEADER_B:])
    return lax.cond(
        over[0] > 0,
        lambda: dense_product(a, b, a_pattern, b_pattern, c_pattern, slots, slot_shift, ahead, row),
        lambda: packed_product(parts, panel, ahead, slots),
    )


def solution(mesh):
    fine = Mesh(mesh.devices.reshape(tuple(SIZES.values())), tuple(SIZES))
    return jax.shard_map(
        local,
        mesh=fine,
        in_specs=(P(ROW, COL),) * 5 + (P(),),
        out_specs=P(ROW, COL),
        check_vma=False,
    )
```

```python
import functools

import jax
import jax.numpy as jnp
from jax import lax
from jax.experimental import pallas as pl
from jax.experimental.pallas import tpu as pltpu
from jax.sharding import Mesh, PartitionSpec as P

SIZES = {"x": 4, "yl": 2, "core": 2, "yh": 2, "z": 4}
ROW = ("x", "yl", "core")
COL = ("yh", "z")
WIDTH = 128
SLICE = 16
CAP = 40
PIECE = 33 * SLICE
PACKED = (CAP + 1) * SLICE
SLICE_B = 32
CAP_B = 42
PIECE_B = 32 * SLICE_B + SLICE
HEADER_B = CAP_B * SLICE_B
PACKED_B = HEADER_B + SLICE
CHUNK = 4
OFFSETS = [(dy, dz) for dy in range(2) for dz in range(4)]


def space(kind):
    return pl.BlockSpec(memory_space=kind)


def from_ahead(value, axis, by):
    n = SIZES[axis]
    return lax.ppermute(value, axis, [((i + by) % n, i) for i in range(n)])


def from_offset(value, offset):
    return lax.ppermute(
        value,
        COL,
        [((y + offset[0]) % 2 * 4 + (z + offset[1]) % 4, y * 4 + z) for y in range(2) for z in range(4)],
    )


def shifted(value, axis, count, shift):
    def branch(by):
        perm = [((i + by) % count, i) for i in range(count)]
        return lambda v: lax.ppermute(v, axis, perm)

    return lax.switch(shift - 1, [branch(by) for by in range(1, count)], value)


def mask_kernel(pattern, ref, out):
    for i in range(4):
        for j in range(8):
            at = (slice(i * WIDTH, (i + 1) * WIDTH), slice(j * WIDTH, (j + 1) * WIDTH))
            block = ref[at]
            out[at] = jnp.where(pattern[i, j] > 0, block, jnp.zeros_like(block))


def masked(value, pattern):
    return pl.pallas_call(
        mask_kernel,
        in_specs=[space(pltpu.SMEM), space(pltpu.VMEM)],
        out_specs=space(pltpu.VMEM),
        out_shape=jax.ShapeDtypeStruct((512, 1024), jnp.bfloat16),
    )(pattern, value)


def flags_as_rows(flags, lane, first=0):
    row = jnp.zeros((SLICE, WIDTH), jnp.float32)
    for i in range(4):
        for j in range(8):
            row = jnp.where(lane == first + i * 8 + j, flags[i, j].astype(jnp.float32), row)
    return row


def cut_kernel(pattern, b_pattern, ref, out):
    lane = lax.broadcasted_iota(jnp.int32, (SLICE, WIDTH), 1)
    row = (flags_as_rows(pattern, lane) + flags_as_rows(b_pattern, lane, 32)).astype(jnp.bfloat16)
    for m in range(8):
        for i in range(4):
            rows = slice(i * WIDTH + m * SLICE, i * WIDTH + (m + 1) * SLICE)
            for j in range(8):
                at = PIECE * m + (i * 8 + j) * SLICE
                out[at : at + SLICE] = ref[rows, j * WIDTH : (j + 1) * WIDTH]
        out[PIECE * m + 32 * SLICE : PIECE * (m + 1)] = row


def cut(value, pattern, b_pattern):
    return pl.pallas_call(
        cut_kernel,
        in_specs=[space(pltpu.SMEM), space(pltpu.SMEM), space(pltpu.VMEM)],
        out_specs=space(pltpu.VMEM),
        out_shape=jax.ShapeDtypeStruct((8 * PIECE, WIDTH), jnp.bfloat16),
    )(pattern, b_pattern, value)


def cut_b_kernel(target, pattern, ref, *outs):
    lane = lax.broadcasted_iota(jnp.int32, (SLICE, WIDTH), 1)
    row = flags_as_rows(pattern, lane).astype(jnp.bfloat16)
    for n, out in enumerate(outs):
        for i in range(4):
            rows = pl.ds(pl.multiple_of(i * WIDTH + target[n] * SLICE_B, SLICE_B), SLICE_B)
            for j in range(8):
                at = (i * 8 + j) * SLICE_B
                out[at : at + SLICE_B] = ref[rows, j * WIDTH : (j + 1) * WIDTH]
        out[32 * SLICE_B : PIECE_B] = row


def cut_b(value, pattern, target):
    return pl.pallas_call(
        cut_b_kernel,
        in_specs=[space(pltpu.SMEM), space(pltpu.SMEM), space(pltpu.VMEM)],
        out_specs=[space(pltpu.VMEM)] * 4,
        out_shape=[jax.ShapeDtypeStruct((PIECE_B, WIDTH), jnp.bfloat16)] * 4,
    )(target, pattern, value)


def pack_a_kernel(slots, c_pattern, pieces, first, second, flags_v, flags_s, place_s, sem):
    packed = (first, second)
    for m in range(8):
        row = pieces[PIECE * m + 32 * SLICE : PIECE * (m + 1)].astype(jnp.float32).astype(jnp.int32)
        flags_v[m : m + 1] = row[0:1]
    copy = pltpu.make_async_copy(flags_v, flags_s, sem)
    copy.start()
    copy.wait()

    def step(n, counts):
        after = []
        for pair in range(2):
            k = n % 64
            at = jnp.where(n < 64, slots[2 * pair], slots[2 * pair + 1]) * 8 + k % 8
            here = flags_s[k // 8, at]
            to = jnp.minimum(counts[pair], CAP)
            packed[pair][pl.ds(pl.multiple_of(to * SLICE, SLICE), SLICE)] = pieces[
                pl.ds(pl.multiple_of(k // 8 * PIECE + at * SLICE, SLICE), SLICE)
            ]
            place_s[k // 8, at] = jnp.where(here > 0, to + 1, 0)
            after.append(counts[pair] + jnp.where(here > 0, 1, 0))
        return tuple(after)

    lax.fori_loop(0, 128, step, (jnp.int32(0), jnp.int32(0)), unroll=8)
    copy = pltpu.make_async_copy(place_s, flags_v, sem)
    copy.start()
    copy.wait()
    lane = lax.broadcasted_iota(jnp.int32, (SLICE, WIDTH), 1)
    sub = lax.broadcasted_iota(jnp.int32, (SLICE, WIDTH), 0)
    kept = flags_as_rows(c_pattern, lane)
    place = flags_v[...].astype(jnp.float32)
    place = jnp.where(lane < 32, jnp.concatenate([place, place], axis=0), jnp.float32(0.0))
    header = jnp.where(sub < 8, place, kept).astype(jnp.bfloat16)
    for ref in packed:
        ref[CAP * SLICE : (CAP + 1) * SLICE] = header


def pack_a(pieces, slots, c_pattern):
    out = jax.ShapeDtypeStruct((PACKED, WIDTH), jnp.bfloat16)
    return pl.pallas_call(
        pack_a_kernel,
        in_specs=[space(pltpu.SMEM)] * 2 + [space(pltpu.VMEM)],
        out_specs=[space(pltpu.VMEM)] * 2,
        out_shape=[out, out],
        scratch_shapes=[
            pltpu.VMEM((8, WIDTH), jnp.int32),
            pltpu.SMEM((8, WIDTH), jnp.int32),
            pltpu.SMEM((8, WIDTH), jnp.int32),
            pltpu.SemaphoreType.DMA,
        ],
    )(slots, c_pattern, pieces)


def pack_b_kernel(source, slots, *refs):
    pieces, pieces_a, packed = refs[:4], refs[4], refs[5]
    held, flags_v, flags_s, place_s, sem = refs[6:]
    flags_v[...] = jnp.zeros_like(flags_v)
    for n in range(4):
        row = pieces[n][32 * SLICE_B : PIECE_B].astype(jnp.float32).astype(jnp.int32)
        flags_v[pl.ds(source[n], 1)] = row[0:1]
    copy = pltpu.make_async_copy(flags_v, flags_s, sem)
    copy.start()
    for n in range(4):
        held[source[n]] = pieces[n][: 32 * SLICE_B]
    copy.wait()

    def step(n, count):
        m, at = n // 32, n % 32
        here = flags_s[m, at]
        to = jnp.minimum(count, CAP_B - 1)
        packed[pl.ds(pl.multiple_of(to * SLICE_B, SLICE_B), SLICE_B)] = held[
            m, pl.ds(pl.multiple_of(at * SLICE_B, SLICE_B), SLICE_B)
        ]
        place_s[m, at] = jnp.where(here > 0, to + 1, 0)
        return count + jnp.where(here > 0, 1, 0)

    lax.fori_loop(0, 128, step, jnp.int32(0), unroll=8)
    copy = pltpu.make_async_copy(place_s, flags_v, sem)
    copy.start()
    copy.wait()
    lane = lax.broadcasted_iota(jnp.int32, (SLICE, WIDTH), 1)
    place = flags_v[...].astype(jnp.float32)
    place = jnp.where((lane < 32) & (lax.broadcasted_iota(jnp.int32, (SLICE, WIDTH), 0) < 4), jnp.concatenate([place, place], axis=0), jnp.float32(0.0))
    in_a = jnp.zeros((SLICE, WIDTH), jnp.float32)
    sub = lax.broadcasted_iota(jnp.int32, (SLICE, WIDTH), 0)
    for m in range(8):
        row = pieces_a[PIECE * m + 32 * SLICE : PIECE * (m + 1)].astype(jnp.float32)
        in_a += row
        place = jnp.where((lane >= 32) & (lane < 64) & (sub == m), row, place)
    counts = []
    for pair in range(2):
        one, two = slots[2 * pair] * 8, slots[2 * pair + 1] * 8
        counted = ((lane >= one) & (lane < one + 8)) | ((lane >= two) & (lane < two + 8))
        counts.append(jnp.sum(jnp.where(counted & (sub == 0), in_a, jnp.float32(0.0))))
    over = jnp.where(jnp.maximum(counts[0], counts[1]) > CAP, jnp.float32(1.0), jnp.float32(0.0))
    packed[HEADER_B:PACKED_B] = jnp.where(sub < 8, place, over).astype(jnp.bfloat16)


def pack_b(pieces, source, pieces_a, slots):
    return pl.pallas_call(
        pack_b_kernel,
        in_specs=[space(pltpu.SMEM)] * 2 + [space(pltpu.VMEM)] * 5,
        out_specs=space(pltpu.VMEM),
        out_shape=jax.ShapeDtypeStruct((PACKED_B, WIDTH), jnp.bfloat16),
        scratch_shapes=[
            pltpu.VMEM((4, 32 * SLICE_B, WIDTH), jnp.bfloat16),
            pltpu.VMEM((8, WIDTH), jnp.int32),
            pltpu.SMEM((8, WIDTH), jnp.int32),
            pltpu.SMEM((8, WIDTH), jnp.int32),
            pltpu.SemaphoreType.DMA,
        ],
    )(source, slots, *pieces, pieces_a)


def over_kernel(headers, over):
    sub = lax.broadcasted_iota(jnp.int32, (SLICE, WIDTH), 0)
    lane = lax.broadcasted_iota(jnp.int32, (SLICE, WIDTH), 1)
    most_a, most_b = jnp.zeros((SLICE, WIDTH), jnp.float32), jnp.zeros((SLICE, 1), jnp.float32)
    for ring in range(4):
        count = jnp.zeros((SLICE, WIDTH), jnp.float32)
        for m in range(4):
            header = headers[m * 4 + ring].astype(jnp.float32)
            count += header
            most_a = jnp.maximum(most_a, header)
        count = jnp.where((lane >= 32) & (lane < 64) & (sub < 8), count, jnp.float32(0.0))
        most_b = jnp.maximum(most_b, jnp.sum(count, axis=1, keepdims=True))
    most_a = jnp.max(jnp.where(sub == 8, most_a, jnp.float32(0.0)))
    over[0] = ((most_a > 0) | (jnp.max(most_b) > CAP_B - 1)).astype(jnp.int32)


def over_capacity(headers):
    return pl.pallas_call(
        over_kernel,
        in_specs=[space(pltpu.VMEM)],
        out_specs=space(pltpu.SMEM),
        out_shape=jax.ShapeDtypeStruct((1,), jnp.int32),
    )(headers)


def product_kernel(source, slots, *refs):
    parts, panel, out = (refs[:4], refs[4:8]), refs[8], refs[9]
    header_v, header_s, listed, rhs, lhs, total, sem = refs[10:]
    for pair in range(2):
        at = CAP * SLICE
        header_v[pair * SLICE : (pair + 1) * SLICE] = parts[pair][0][at : at + SLICE].astype(jnp.float32).astype(jnp.int32)
    for n in range(4):
        at = n * PACKED_B + HEADER_B
        header_v[(2 + n) * SLICE : (3 + n) * SLICE] = panel[at : at + SLICE].astype(jnp.float32).astype(jnp.int32)
    copy = pltpu.make_async_copy(header_v, header_s, sem)
    copy.start()
    copy.wait()

    length = jnp.int32(0)
    chunks = []
    for pair in range(2):
        q0, q1 = slots[2 * pair], slots[2 * pair + 1]

        def step(k, length, pair=pair, q0=q0, q1=q1):
            first = header_s[pair * SLICE + k // 8, q0 * 8 + k % 8]
            second = header_s[pair * SLICE + k // 8, q1 * 8 + k % 8]
            listed[0, length] = k
            listed[1, length] = first
            listed[2, length] = second
            return length + jnp.where(first + second > 0, 1, 0)

        length = lax.fori_loop(0, 64, step, length, unroll=8)
        for i in range(CHUNK - 1):
            for n in range(3):
                listed[n, length + i] = 0
        length = (length + CHUNK - 1) // CHUNK * CHUNK
        chunks.append(length // CHUNK)
    total[...] = jnp.zeros_like(total)

    def multiply(chunk, carry, pair):
        for i in range(CHUNK):
            for slot in range(2):
                place = listed[1 + slot, chunk * CHUNK + i]
                at = jnp.maximum(place - 1, 0) * SLICE
                for dy in range(2):
                    for step in range(4):
                        value = parts[pair][step][pl.ds(pl.multiple_of(at + dy * PACKED, SLICE), SLICE)]
                        rows = pl.ds(pl.multiple_of(slot * WIDTH + source[dy * 4 + step] * SLICE, SLICE), SLICE)
                        lhs[rows, i * WIDTH : (i + 1) * WIDTH] = jnp.where(place > 0, value, jnp.zeros_like(value))
            k = listed[0, chunk * CHUNK + i]
            ring = k // 4 % 4
            for j in range(8):
                place = header_s[(2 + ring) * SLICE + k // 16, k % 4 * 8 + j]
                at = ring * PACKED_B + jnp.maximum(place - 1, 0) * SLICE_B
                for m in range(4):
                    value = panel[pl.ds(pl.multiple_of(at + m * 4 * PACKED_B, SLICE), SLICE_B)]
                    rhs[i * WIDTH + m * SLICE_B : i * WIDTH + (m + 1) * SLICE_B, j * WIDTH : (j + 1) * WIDTH] = jnp.where(
                        place > 0, value, jnp.zeros_like(value)
                    )
        for n in range(4):
            cols = slice(n * 256, (n + 1) * 256)
            total[pair, :, cols] += jnp.dot(lhs[...], rhs[:, cols], preferred_element_type=jnp.float32)
        return carry

    lax.fori_loop(0, chunks[0], functools.partial(multiply, pair=0), 0)
    lax.fori_loop(chunks[0], chunks[1], functools.partial(multiply, pair=1), 0)
    for slot in range(4):
        q = slots[slot]
        rows = slice(slot % 2 * WIDTH, (slot % 2 + 1) * WIDTH)
        for j in range(8):
            block = total[slot // 2, rows, j * WIDTH : (j + 1) * WIDTH]
            out[slot * WIDTH : (slot + 1) * WIDTH, j * WIDTH : (j + 1) * WIDTH] = jnp.where(
                header_s[slot // 2 * SLICE + 8, q * 8 + j] > 0, block, jnp.zeros_like(block)
            ).astype(jnp.bfloat16)


def packed_product(parts, panel, source, slots):
    return pl.pallas_call(
        product_kernel,
        in_specs=[space(pltpu.SMEM)] * 2 + [space(pltpu.VMEM)] * 9,
        out_specs=space(pltpu.VMEM),
        out_shape=jax.ShapeDtypeStruct((512, 1024), jnp.bfloat16),
        scratch_shapes=[
            pltpu.VMEM((6 * SLICE, WIDTH), jnp.int32),
            pltpu.SMEM((6 * SLICE, WIDTH), jnp.int32),
            pltpu.SMEM((3, 2 * 64 + 2 * CHUNK), jnp.int32),
            pltpu.VMEM((CHUNK * WIDTH, 1024), jnp.bfloat16),
            pltpu.VMEM((2 * WIDTH, CHUNK * WIDTH), jnp.bfloat16),
            pltpu.VMEM((2, 2 * WIDTH, 1024), jnp.float32),
            pltpu.SemaphoreType.DMA,
        ],
        compiler_params=pltpu.CompilerParams(vmem_limit_bytes=24 * 2**20),
    )(source, slots, *parts, panel)


def dense_product(a, b, a_pattern, b_pattern, c_pattern, slots, slot_shift, source, row):
    value = masked(a, a_pattern)
    moved, kept = [], []
    for pair in range(2):
        rows = [lax.dynamic_slice_in_dim(value, slots[2 * pair + t] * WIDTH, WIDTH, 0) for t in range(2)]
        flags = [lax.dynamic_slice_in_dim(c_pattern, slots[2 * pair + t], 1, 0) for t in range(2)]
        moved.append(shifted(jnp.concatenate(rows, axis=0), ROW, 16, slot_shift[2 * pair]))
        kept.append(shifted(jnp.concatenate(flags, axis=0), ROW, 16, slot_shift[2 * pair]))
    value = jnp.concatenate(moved, axis=0)
    full = jnp.zeros((512, 8192), jnp.bfloat16)
    for t, offset in enumerate(OFFSETS):
        piece = from_offset(value, offset) if t else value
        full = lax.dynamic_update_slice(full, piece, (0, source[t] * 1024))
    own_b = masked(b, b_pattern)
    panel = jnp.zeros((8192, 1024), jnp.bfloat16)
    for by in range(16):
        piece = lax.ppermute(own_b, ROW, [((i + by) % 16, i) for i in range(16)]) if by else own_b
        panel = lax.dynamic_update_slice(panel, piece, ((row + by) % 16 * 512, 0))
    product = jnp.dot(full, panel, preferred_element_type=jnp.float32)
    mask = jnp.repeat(jnp.repeat(jnp.concatenate(kept, axis=0), WIDTH, axis=0), WIDTH, axis=1)
    return jnp.where(mask > 0, product, jnp.float32(0.0)).astype(jnp.bfloat16)


def local(a, b, a_pattern, b_pattern, c_pattern, owner_list):
    slot_shift = owner_list[:4] // 4 % 16
    slots = owner_list[:4] % 4
    yh, z = lax.axis_index("yh").astype(jnp.int32), lax.axis_index("z").astype(jnp.int32)
    row = lax.axis_index(ROW).astype(jnp.int32)
    ahead = jnp.stack([(yh + dy) % 2 * 4 + (z + dz) % 4 for dy, dz in OFFSETS])
    cut_a = cut(a, a_pattern, b_pattern)
    b_after, _ = lax.optimization_barrier((b, cut_a))
    pieces_a = lax.all_to_all(cut_a, COL, 0, 0, tiled=True)
    x = lax.axis_index("x").astype(jnp.int32)
    pieces_b = cut_b(b_after, b_pattern, jnp.stack([(x - n) % 4 for n in range(4)]))
    pieces_b = [from_ahead(piece, "x", n) if n else piece for n, piece in enumerate(pieces_b)]
    first, second = pack_a(pieces_a, slots, c_pattern)
    pieces_b, _ = lax.optimization_barrier((pieces_b, first))
    packed_b = pack_b(pieces_b, jnp.stack([(x + n) % 4 for n in range(4)]), pieces_a, slots)
    panel = lax.all_gather(packed_b, ROW, axis=0, tiled=True)
    parts = []
    for pair, packed in enumerate((first, second)):
        moved = shifted(packed, ROW, 16, slot_shift[2 * pair])
        both = jnp.concatenate([moved, from_ahead(moved, "yh", 1)], axis=0)
        parts += [both] + [from_ahead(both, "z", step) for step in (1, 2, 3)]
    over = over_capacity(panel.reshape(16, PACKED_B, WIDTH)[:, HEADER_B:])
    return lax.cond(
        over[0] > 0,
        lambda: dense_product(a, b, a_pattern, b_pattern, c_pattern, slots, slot_shift, ahead, row),
        lambda: packed_product(parts, panel, ahead, slots),
    )


def solution(mesh):
    fine = Mesh(mesh.devices.reshape(tuple(SIZES.values())), tuple(SIZES))
    return jax.shard_map(
        local,
        mesh=fine,
        in_specs=(P(ROW, COL),) * 5 + (P(),),
        out_specs=P(ROW, COL),
        check_vma=False,
    )
```

```python
import functools

import jax
import jax.numpy as jnp
from jax import lax
from jax.experimental import pallas as pl
from jax.experimental.pallas import tpu as pltpu
from jax.sharding import Mesh, PartitionSpec as P

SIZES = {"x": 4, "yl": 2, "core": 2, "yh": 2, "z": 4}
ROW = ("x", "yl", "core")
COL = ("yh", "z")
WIDTH = 128
SLICE = 16
CAP = 38
PIECE = 33 * SLICE
PACKED = (CAP + 1) * SLICE
SLICE_B = 32
CAP_B = 42
PIECE_B = 32 * SLICE_B + SLICE
HEADER_B = CAP_B * SLICE_B
PACKED_B = HEADER_B + SLICE
CHUNK = 4
OFFSETS = [(dy, dz) for dy in range(2) for dz in range(4)]


def space(kind):
    return pl.BlockSpec(memory_space=kind)


def from_ahead(value, axis, by):
    n = SIZES[axis]
    return lax.ppermute(value, axis, [((i + by) % n, i) for i in range(n)])


def from_offset(value, offset):
    return lax.ppermute(
        value,
        COL,
        [((y + offset[0]) % 2 * 4 + (z + offset[1]) % 4, y * 4 + z) for y in range(2) for z in range(4)],
    )


def shifted(value, axis, count, shift):
    def branch(by):
        perm = [((i + by) % count, i) for i in range(count)]
        return lambda v: lax.ppermute(v, axis, perm)

    return lax.switch(shift - 1, [branch(by) for by in range(1, count)], value)


def mask_kernel(pattern, ref, out):
    for i in range(4):
        for j in range(8):
            at = (slice(i * WIDTH, (i + 1) * WIDTH), slice(j * WIDTH, (j + 1) * WIDTH))
            block = ref[at]
            out[at] = jnp.where(pattern[i, j] > 0, block, jnp.zeros_like(block))


def masked(value, pattern):
    return pl.pallas_call(
        mask_kernel,
        in_specs=[space(pltpu.SMEM), space(pltpu.VMEM)],
        out_specs=space(pltpu.VMEM),
        out_shape=jax.ShapeDtypeStruct((512, 1024), jnp.bfloat16),
    )(pattern, value)


def flags_as_rows(flags, lane, first=0):
    row = jnp.zeros((SLICE, WIDTH), jnp.float32)
    for i in range(4):
        for j in range(8):
            row = jnp.where(lane == first + i * 8 + j, flags[i, j].astype(jnp.float32), row)
    return row


def cut_kernel(pattern, b_pattern, ref, out):
    lane = lax.broadcasted_iota(jnp.int32, (SLICE, WIDTH), 1)
    row = (flags_as_rows(pattern, lane) + flags_as_rows(b_pattern, lane, 32)).astype(jnp.bfloat16)
    for m in range(8):
        for i in range(4):
            rows = slice(i * WIDTH + m * SLICE, i * WIDTH + (m + 1) * SLICE)
            for j in range(8):
                at = PIECE * m + (i * 8 + j) * SLICE
                out[at : at + SLICE] = ref[rows, j * WIDTH : (j + 1) * WIDTH]
        out[PIECE * m + 32 * SLICE : PIECE * (m + 1)] = row


def cut(value, pattern, b_pattern):
    return pl.pallas_call(
        cut_kernel,
        in_specs=[space(pltpu.SMEM), space(pltpu.SMEM), space(pltpu.VMEM)],
        out_specs=space(pltpu.VMEM),
        out_shape=jax.ShapeDtypeStruct((8 * PIECE, WIDTH), jnp.bfloat16),
    )(pattern, b_pattern, value)


def cut_b_kernel(target, pattern, ref, *outs):
    lane = lax.broadcasted_iota(jnp.int32, (SLICE, WIDTH), 1)
    row = flags_as_rows(pattern, lane).astype(jnp.bfloat16)
    for n, out in enumerate(outs):
        for i in range(4):
            rows = pl.ds(pl.multiple_of(i * WIDTH + target[n] * SLICE_B, SLICE_B), SLICE_B)
            for j in range(8):
                at = (i * 8 + j) * SLICE_B
                out[at : at + SLICE_B] = ref[rows, j * WIDTH : (j + 1) * WIDTH]
        out[32 * SLICE_B : PIECE_B] = row


def cut_b(value, pattern, target):
    return pl.pallas_call(
        cut_b_kernel,
        in_specs=[space(pltpu.SMEM), space(pltpu.SMEM), space(pltpu.VMEM)],
        out_specs=[space(pltpu.VMEM)] * 4,
        out_shape=[jax.ShapeDtypeStruct((PIECE_B, WIDTH), jnp.bfloat16)] * 4,
    )(target, pattern, value)


def pack_a_kernel(slots, c_pattern, pieces, first, second, flags_v, flags_s, place_s, sem):
    packed = (first, second)
    for m in range(8):
        row = pieces[PIECE * m + 32 * SLICE : PIECE * (m + 1)].astype(jnp.float32).astype(jnp.int32)
        flags_v[m : m + 1] = row[0:1]
    copy = pltpu.make_async_copy(flags_v, flags_s, sem)
    copy.start()
    copy.wait()

    def step(n, counts):
        after = []
        for pair in range(2):
            k = n % 64
            at = jnp.where(n < 64, slots[2 * pair], slots[2 * pair + 1]) * 8 + k % 8
            here = flags_s[k // 8, at]
            to = jnp.minimum(counts[pair], CAP)
            packed[pair][pl.ds(pl.multiple_of(to * SLICE, SLICE), SLICE)] = pieces[
                pl.ds(pl.multiple_of(k // 8 * PIECE + at * SLICE, SLICE), SLICE)
            ]
            place_s[k // 8, at] = jnp.where(here > 0, to + 1, 0)
            after.append(counts[pair] + jnp.where(here > 0, 1, 0))
        return tuple(after)

    lax.fori_loop(0, 128, step, (jnp.int32(0), jnp.int32(0)), unroll=8)
    copy = pltpu.make_async_copy(place_s, flags_v, sem)
    copy.start()
    copy.wait()
    lane = lax.broadcasted_iota(jnp.int32, (SLICE, WIDTH), 1)
    sub = lax.broadcasted_iota(jnp.int32, (SLICE, WIDTH), 0)
    kept = flags_as_rows(c_pattern, lane)
    place = flags_v[...].astype(jnp.float32)
    place = jnp.where(lane < 32, jnp.concatenate([place, place], axis=0), jnp.float32(0.0))
    header = jnp.where(sub < 8, place, kept).astype(jnp.bfloat16)
    for ref in packed:
        ref[CAP * SLICE : (CAP + 1) * SLICE] = header


def pack_a(pieces, slots, c_pattern):
    out = jax.ShapeDtypeStruct((PACKED, WIDTH), jnp.bfloat16)
    return pl.pallas_call(
        pack_a_kernel,
        in_specs=[space(pltpu.SMEM)] * 2 + [space(pltpu.VMEM)],
        out_specs=[space(pltpu.VMEM)] * 2,
        out_shape=[out, out],
        scratch_shapes=[
            pltpu.VMEM((8, WIDTH), jnp.int32),
            pltpu.SMEM((8, WIDTH), jnp.int32),
            pltpu.SMEM((8, WIDTH), jnp.int32),
            pltpu.SemaphoreType.DMA,
        ],
    )(slots, c_pattern, pieces)


def pack_b_kernel(source, slots, *refs):
    pieces, pieces_a, packed = refs[:4], refs[4], refs[5]
    held, flags_v, flags_s, place_s, sem = refs[6:]
    flags_v[...] = jnp.zeros_like(flags_v)
    for n in range(4):
        row = pieces[n][32 * SLICE_B : PIECE_B].astype(jnp.float32).astype(jnp.int32)
        flags_v[pl.ds(source[n], 1)] = row[0:1]
    copy = pltpu.make_async_copy(flags_v, flags_s, sem)
    copy.start()
    for n in range(4):
        held[source[n]] = pieces[n][: 32 * SLICE_B]
    copy.wait()

    def step(n, count):
        m, at = n // 32, n % 32
        here = flags_s[m, at]
        to = jnp.minimum(count, CAP_B - 1)
        packed[pl.ds(pl.multiple_of(to * SLICE_B, SLICE_B), SLICE_B)] = held[
            m, pl.ds(pl.multiple_of(at * SLICE_B, SLICE_B), SLICE_B)
        ]
        place_s[m, at] = jnp.where(here > 0, to + 1, 0)
        return count + jnp.where(here > 0, 1, 0)

    lax.fori_loop(0, 128, step, jnp.int32(0), unroll=8)
    copy = pltpu.make_async_copy(place_s, flags_v, sem)
    copy.start()
    copy.wait()
    lane = lax.broadcasted_iota(jnp.int32, (SLICE, WIDTH), 1)
    place = flags_v[...].astype(jnp.float32)
    place = jnp.where((lane < 32) & (lax.broadcasted_iota(jnp.int32, (SLICE, WIDTH), 0) < 4), jnp.concatenate([place, place], axis=0), jnp.float32(0.0))
    in_a = jnp.zeros((SLICE, WIDTH), jnp.float32)
    sub = lax.broadcasted_iota(jnp.int32, (SLICE, WIDTH), 0)
    for m in range(8):
        row = pieces_a[PIECE * m + 32 * SLICE : PIECE * (m + 1)].astype(jnp.float32)
        in_a += row
        place = jnp.where((lane >= 32) & (lane < 64) & (sub == m), row, place)
    counts = []
    for pair in range(2):
        one, two = slots[2 * pair] * 8, slots[2 * pair + 1] * 8
        counted = ((lane >= one) & (lane < one + 8)) | ((lane >= two) & (lane < two + 8))
        counts.append(jnp.sum(jnp.where(counted & (sub == 0), in_a, jnp.float32(0.0))))
    over = jnp.where(jnp.maximum(counts[0], counts[1]) > CAP, jnp.float32(1.0), jnp.float32(0.0))
    packed[HEADER_B:PACKED_B] = jnp.where(sub < 8, place, over).astype(jnp.bfloat16)


def pack_b(pieces, source, pieces_a, slots):
    return pl.pallas_call(
        pack_b_kernel,
        in_specs=[space(pltpu.SMEM)] * 2 + [space(pltpu.VMEM)] * 5,
        out_specs=space(pltpu.VMEM),
        out_shape=jax.ShapeDtypeStruct((PACKED_B, WIDTH), jnp.bfloat16),
        scratch_shapes=[
            pltpu.VMEM((4, 32 * SLICE_B, WIDTH), jnp.bfloat16),
            pltpu.VMEM((8, WIDTH), jnp.int32),
            pltpu.SMEM((8, WIDTH), jnp.int32),
            pltpu.SMEM((8, WIDTH), jnp.int32),
            pltpu.SemaphoreType.DMA,
        ],
    )(source, slots, *pieces, pieces_a)


def over_kernel(headers, over):
    sub = lax.broadcasted_iota(jnp.int32, (SLICE, WIDTH), 0)
    lane = lax.broadcasted_iota(jnp.int32, (SLICE, WIDTH), 1)
    most_a, most_b = jnp.zeros((SLICE, WIDTH), jnp.float32), jnp.zeros((SLICE, 1), jnp.float32)
    for ring in range(4):
        count = jnp.zeros((SLICE, WIDTH), jnp.float32)
        for m in range(4):
            header = headers[m * 4 + ring].astype(jnp.float32)
            count += header
            most_a = jnp.maximum(most_a, header)
        count = jnp.where((lane >= 32) & (lane < 64) & (sub < 8), count, jnp.float32(0.0))
        most_b = jnp.maximum(most_b, jnp.sum(count, axis=1, keepdims=True))
    most_a = jnp.max(jnp.where(sub == 8, most_a, jnp.float32(0.0)))
    over[0] = ((most_a > 0) | (jnp.max(most_b) > CAP_B - 1)).astype(jnp.int32)


def over_capacity(headers):
    return pl.pallas_call(
        over_kernel,
        in_specs=[space(pltpu.VMEM)],
        out_specs=space(pltpu.SMEM),
        out_shape=jax.ShapeDtypeStruct((1,), jnp.int32),
    )(headers)


def product_kernel(source, slots, *refs):
    panel, out = refs[10], refs[11]
    header_v, header_s, listed, rhs, lhs, total, sem = refs[12:]
    parts = [
        [[(r[0], dy * PACKED), (r[1], dy * PACKED), (r[3 + dy], 0), (r[2], dy * PACKED)] for dy in range(2)]
        for r in (refs[:5], refs[5:10])
    ]
    for pair in range(2):
        at = CAP * SLICE
        header_v[pair * SLICE : (pair + 1) * SLICE] = parts[pair][0][0][0][at : at + SLICE].astype(jnp.float32).astype(jnp.int32)
    for n in range(4):
        at = n * PACKED_B + HEADER_B
        header_v[(2 + n) * SLICE : (3 + n) * SLICE] = panel[at : at + SLICE].astype(jnp.float32).astype(jnp.int32)
    copy = pltpu.make_async_copy(header_v, header_s, sem)
    copy.start()
    copy.wait()

    length = jnp.int32(0)
    chunks = []
    for pair in range(2):
        q0, q1 = slots[2 * pair], slots[2 * pair + 1]

        def step(k, length, pair=pair, q0=q0, q1=q1):
            first = header_s[pair * SLICE + k // 8, q0 * 8 + k % 8]
            second = header_s[pair * SLICE + k // 8, q1 * 8 + k % 8]
            listed[0, length] = k
            listed[1, length] = first
            listed[2, length] = second
            return length + jnp.where(first + second > 0, 1, 0)

        length = lax.fori_loop(0, 64, step, length, unroll=8)
        for i in range(CHUNK - 1):
            for n in range(3):
                listed[n, length + i] = 0
        length = (length + CHUNK - 1) // CHUNK * CHUNK
        chunks.append(length // CHUNK)
    total[...] = jnp.zeros_like(total)

    def multiply(chunk, carry, pair):
        for i in range(CHUNK):
            for slot in range(2):
                place = listed[1 + slot, chunk * CHUNK + i]
                at = jnp.maximum(place - 1, 0) * SLICE
                for dy in range(2):
                    for step in range(4):
                        part, begin = parts[pair][dy][step]
                        value = part[pl.ds(pl.multiple_of(at + begin, SLICE), SLICE)]
                        rows = pl.ds(pl.multiple_of(slot * WIDTH + source[dy * 4 + step] * SLICE, SLICE), SLICE)
                        lhs[rows, i * WIDTH : (i + 1) * WIDTH] = jnp.where(place > 0, value, jnp.zeros_like(value))
            k = listed[0, chunk * CHUNK + i]
            ring = k // 4 % 4
            for j in range(8):
                place = header_s[(2 + ring) * SLICE + k // 16, k % 4 * 8 + j]
                at = ring * PACKED_B + jnp.maximum(place - 1, 0) * SLICE_B
                for m in range(4):
                    value = panel[pl.ds(pl.multiple_of(at + m * 4 * PACKED_B, SLICE), SLICE_B)]
                    rhs[i * WIDTH + m * SLICE_B : i * WIDTH + (m + 1) * SLICE_B, j * WIDTH : (j + 1) * WIDTH] = jnp.where(
                        place > 0, value, jnp.zeros_like(value)
                    )
        for n in range(4):
            cols = slice(n * 256, (n + 1) * 256)
            total[pair, :, cols] += jnp.dot(lhs[...], rhs[:, cols], preferred_element_type=jnp.float32)
        return carry

    lax.fori_loop(0, chunks[0], functools.partial(multiply, pair=0), 0)
    lax.fori_loop(chunks[0], chunks[1], functools.partial(multiply, pair=1), 0)
    for slot in range(4):
        q = slots[slot]
        rows = slice(slot % 2 * WIDTH, (slot % 2 + 1) * WIDTH)
        for j in range(8):
            block = total[slot // 2, rows, j * WIDTH : (j + 1) * WIDTH]
            out[slot * WIDTH : (slot + 1) * WIDTH, j * WIDTH : (j + 1) * WIDTH] = jnp.where(
                header_s[slot // 2 * SLICE + 8, q * 8 + j] > 0, block, jnp.zeros_like(block)
            ).astype(jnp.bfloat16)


def packed_product(parts, panel, source, slots):
    return pl.pallas_call(
        product_kernel,
        in_specs=[space(pltpu.SMEM)] * 2 + [space(pltpu.VMEM)] * 11,
        out_specs=space(pltpu.VMEM),
        out_shape=jax.ShapeDtypeStruct((512, 1024), jnp.bfloat16),
        scratch_shapes=[
            pltpu.VMEM((6 * SLICE, WIDTH), jnp.int32),
            pltpu.SMEM((6 * SLICE, WIDTH), jnp.int32),
            pltpu.SMEM((3, 2 * 64 + 2 * CHUNK), jnp.int32),
            pltpu.VMEM((CHUNK * WIDTH, 1024), jnp.bfloat16),
            pltpu.VMEM((2 * WIDTH, CHUNK * WIDTH), jnp.bfloat16),
            pltpu.VMEM((2, 2 * WIDTH, 1024), jnp.float32),
            pltpu.SemaphoreType.DMA,
        ],
        compiler_params=pltpu.CompilerParams(vmem_limit_bytes=24 * 2**20),
    )(source, slots, *parts, panel)


def dense_product(a, b, a_pattern, b_pattern, c_pattern, slots, slot_shift, source, row):
    value = masked(a, a_pattern)
    moved, kept = [], []
    for pair in range(2):
        rows = [lax.dynamic_slice_in_dim(value, slots[2 * pair + t] * WIDTH, WIDTH, 0) for t in range(2)]
        flags = [lax.dynamic_slice_in_dim(c_pattern, slots[2 * pair + t], 1, 0) for t in range(2)]
        moved.append(shifted(jnp.concatenate(rows, axis=0), ROW, 16, slot_shift[2 * pair]))
        kept.append(shifted(jnp.concatenate(flags, axis=0), ROW, 16, slot_shift[2 * pair]))
    value = jnp.concatenate(moved, axis=0)
    full = jnp.zeros((512, 8192), jnp.bfloat16)
    for t, offset in enumerate(OFFSETS):
        piece = from_offset(value, offset) if t else value
        full = lax.dynamic_update_slice(full, piece, (0, source[t] * 1024))
    own_b = masked(b, b_pattern)
    panel = jnp.zeros((8192, 1024), jnp.bfloat16)
    for by in range(16):
        piece = lax.ppermute(own_b, ROW, [((i + by) % 16, i) for i in range(16)]) if by else own_b
        panel = lax.dynamic_update_slice(panel, piece, ((row + by) % 16 * 512, 0))
    product = jnp.dot(full, panel, preferred_element_type=jnp.float32)
    mask = jnp.repeat(jnp.repeat(jnp.concatenate(kept, axis=0), WIDTH, axis=0), WIDTH, axis=1)
    return jnp.where(mask > 0, product, jnp.float32(0.0)).astype(jnp.bfloat16)


def local(a, b, a_pattern, b_pattern, c_pattern, owner_list):
    slot_shift = owner_list[:4] // 4 % 16
    slots = owner_list[:4] % 4
    yh, z = lax.axis_index("yh").astype(jnp.int32), lax.axis_index("z").astype(jnp.int32)
    row = lax.axis_index(ROW).astype(jnp.int32)
    ahead = jnp.stack([(yh + dy) % 2 * 4 + (z + dz) % 4 for dy, dz in OFFSETS])
    cut_a = cut(a, a_pattern, b_pattern)
    b_after, _ = lax.optimization_barrier((b, cut_a))
    pieces_a = lax.all_to_all(cut_a, COL, 0, 0, tiled=True)
    x = lax.axis_index("x").astype(jnp.int32)
    pieces_b = cut_b(b_after, b_pattern, jnp.stack([(x - n) % 4 for n in range(4)]))
    pieces_b = [from_ahead(piece, "x", n) if n else piece for n, piece in enumerate(pieces_b)]
    first, second = pack_a(pieces_a, slots, c_pattern)
    pieces_b, _ = lax.optimization_barrier((pieces_b, first))
    packed_b = pack_b(pieces_b, jnp.stack([(x + n) % 4 for n in range(4)]), pieces_a, slots)
    panel = lax.all_gather(packed_b, ROW, axis=0, tiled=True)
    parts = []
    for pair, packed in enumerate((first, second)):
        moved = shifted(packed, ROW, 16, slot_shift[2 * pair])
        both = jnp.concatenate([moved, from_ahead(moved, "yh", 1)], axis=0)
        near = [from_ahead(both, "z", step) for step in (1, 3)]
        far = [from_ahead(near[0][:PACKED], "z", 1), from_ahead(near[1][PACKED:], "z", 3)]
        parts += [both, *near, *far]
    over = over_capacity(panel.reshape(16, PACKED_B, WIDTH)[:, HEADER_B:])
    return lax.cond(
        over[0] > 0,
        lambda: dense_product(a, b, a_pattern, b_pattern, c_pattern, slots, slot_shift, ahead, row),
        lambda: packed_product(parts, panel, ahead, slots),
    )


def solution(mesh):
    fine = Mesh(mesh.devices.reshape(tuple(SIZES.values())), tuple(SIZES))
    return jax.shard_map(
        local,
        mesh=fine,
        in_specs=(P(ROW, COL),) * 5 + (P(),),
        out_specs=P(ROW, COL),
        check_vma=False,
    )
```

```python
import functools

import jax
import jax.numpy as jnp
from jax import lax
from jax.experimental import pallas as pl
from jax.experimental.pallas import tpu as pltpu
from jax.sharding import Mesh, PartitionSpec as P

SIZES = {"x": 4, "yl": 2, "core": 2, "yh": 2, "z": 4}
ROW = ("x", "yl", "core")
COL = ("yh", "z")
WIDTH = 128
SLICE = 16
CAP = 38
PIECE = 33 * SLICE
PACKED = (CAP + 1) * SLICE
SLICE_B = 32
CAP_B = 42
PIECE_B = 32 * SLICE_B + SLICE
HEADER_B = CAP_B * SLICE_B
PACKED_B = HEADER_B + SLICE
CHUNK = 4
OFFSETS = [(dy, dz) for dy in range(2) for dz in range(4)]


def space(kind):
    return pl.BlockSpec(memory_space=kind)


def from_ahead(value, axis, by):
    n = SIZES[axis]
    return lax.ppermute(value, axis, [((i + by) % n, i) for i in range(n)])


def from_offset(value, offset):
    return lax.ppermute(
        value,
        COL,
        [((y + offset[0]) % 2 * 4 + (z + offset[1]) % 4, y * 4 + z) for y in range(2) for z in range(4)],
    )


def shifted(value, axis, count, shift):
    def branch(by):
        perm = [((i + by) % count, i) for i in range(count)]
        return lambda v: lax.ppermute(v, axis, perm)

    return lax.switch(shift - 1, [branch(by) for by in range(1, count)], value)


def mask_kernel(pattern, ref, out):
    for i in range(4):
        for j in range(8):
            at = (slice(i * WIDTH, (i + 1) * WIDTH), slice(j * WIDTH, (j + 1) * WIDTH))
            block = ref[at]
            out[at] = jnp.where(pattern[i, j] > 0, block, jnp.zeros_like(block))


def masked(value, pattern):
    return pl.pallas_call(
        mask_kernel,
        in_specs=[space(pltpu.SMEM), space(pltpu.VMEM)],
        out_specs=space(pltpu.VMEM),
        out_shape=jax.ShapeDtypeStruct((512, 1024), jnp.bfloat16),
    )(pattern, value)


def flags_as_rows(flags, lane, first=0):
    row = jnp.zeros((SLICE, WIDTH), jnp.float32)
    for i in range(4):
        for j in range(8):
            row = jnp.where(lane == first + i * 8 + j, flags[i, j].astype(jnp.float32), row)
    return row


def cut_kernel(pattern, b_pattern, ref, out):
    lane = lax.broadcasted_iota(jnp.int32, (SLICE, WIDTH), 1)
    row = (flags_as_rows(pattern, lane) + flags_as_rows(b_pattern, lane, 32)).astype(jnp.bfloat16)
    for m in range(8):
        for i in range(4):
            rows = slice(i * WIDTH + m * SLICE, i * WIDTH + (m + 1) * SLICE)
            for j in range(8):
                at = PIECE * m + (i * 8 + j) * SLICE
                out[at : at + SLICE] = ref[rows, j * WIDTH : (j + 1) * WIDTH]
        out[PIECE * m + 32 * SLICE : PIECE * (m + 1)] = row


def cut(value, pattern, b_pattern):
    return pl.pallas_call(
        cut_kernel,
        in_specs=[space(pltpu.SMEM), space(pltpu.SMEM), space(pltpu.VMEM)],
        out_specs=space(pltpu.VMEM),
        out_shape=jax.ShapeDtypeStruct((8 * PIECE, WIDTH), jnp.bfloat16),
    )(pattern, b_pattern, value)


def cut_b_kernel(target, pattern, ref, *outs):
    lane = lax.broadcasted_iota(jnp.int32, (SLICE, WIDTH), 1)
    row = flags_as_rows(pattern, lane).astype(jnp.bfloat16)
    for n, out in enumerate(outs):
        for i in range(4):
            rows = pl.ds(pl.multiple_of(i * WIDTH + target[n] * SLICE_B, SLICE_B), SLICE_B)
            for j in range(8):
                at = (i * 8 + j) * SLICE_B
                out[at : at + SLICE_B] = ref[rows, j * WIDTH : (j + 1) * WIDTH]
        out[32 * SLICE_B : PIECE_B] = row


def cut_b(value, pattern, target):
    return pl.pallas_call(
        cut_b_kernel,
        in_specs=[space(pltpu.SMEM), space(pltpu.SMEM), space(pltpu.VMEM)],
        out_specs=[space(pltpu.VMEM)] * 4,
        out_shape=[jax.ShapeDtypeStruct((PIECE_B, WIDTH), jnp.bfloat16)] * 4,
    )(target, pattern, value)


def pack_a_kernel(slots, c_pattern, pieces, first, second, flags_v, flags_s, place_s, sem):
    packed = (first, second)
    for m in range(8):
        row = pieces[PIECE * m + 32 * SLICE : PIECE * (m + 1)].astype(jnp.float32).astype(jnp.int32)
        flags_v[m : m + 1] = row[0:1]
    copy = pltpu.make_async_copy(flags_v, flags_s, sem)
    copy.start()
    copy.wait()

    def step(n, counts):
        after = []
        for pair in range(2):
            k = n % 64
            at = jnp.where(n < 64, slots[2 * pair], slots[2 * pair + 1]) * 8 + k % 8
            here = flags_s[k // 8, at]
            to = jnp.minimum(counts[pair], CAP)
            packed[pair][pl.ds(pl.multiple_of(to * SLICE, SLICE), SLICE)] = pieces[
                pl.ds(pl.multiple_of(k // 8 * PIECE + at * SLICE, SLICE), SLICE)
            ]
            place_s[k // 8, at] = jnp.where(here > 0, to + 1, 0)
            after.append(counts[pair] + jnp.where(here > 0, 1, 0))
        return tuple(after)

    lax.fori_loop(0, 128, step, (jnp.int32(0), jnp.int32(0)), unroll=8)
    copy = pltpu.make_async_copy(place_s, flags_v, sem)
    copy.start()
    copy.wait()
    lane = lax.broadcasted_iota(jnp.int32, (SLICE, WIDTH), 1)
    sub = lax.broadcasted_iota(jnp.int32, (SLICE, WIDTH), 0)
    kept = flags_as_rows(c_pattern, lane)
    place = flags_v[...].astype(jnp.float32)
    place = jnp.where(lane < 32, jnp.concatenate([place, place], axis=0), jnp.float32(0.0))
    header = jnp.where(sub < 8, place, kept).astype(jnp.bfloat16)
    for ref in packed:
        ref[CAP * SLICE : (CAP + 1) * SLICE] = header


def pack_a(pieces, slots, c_pattern):
    out = jax.ShapeDtypeStruct((PACKED, WIDTH), jnp.bfloat16)
    return pl.pallas_call(
        pack_a_kernel,
        in_specs=[space(pltpu.SMEM)] * 2 + [space(pltpu.VMEM)],
        out_specs=[space(pltpu.VMEM)] * 2,
        out_shape=[out, out],
        scratch_shapes=[
            pltpu.VMEM((8, WIDTH), jnp.int32),
            pltpu.SMEM((8, WIDTH), jnp.int32),
            pltpu.SMEM((8, WIDTH), jnp.int32),
            pltpu.SemaphoreType.DMA,
        ],
    )(slots, c_pattern, pieces)


def pack_b_kernel(source, slots, *refs):
    pieces, pieces_a, packed = refs[:4], refs[4], refs[5]
    held, flags_v, flags_s, place_s, sem = refs[6:]
    flags_v[...] = jnp.zeros_like(flags_v)
    for n in range(4):
        row = pieces[n][32 * SLICE_B : PIECE_B].astype(jnp.float32).astype(jnp.int32)
        flags_v[pl.ds(source[n], 1)] = row[0:1]
    copy = pltpu.make_async_copy(flags_v, flags_s, sem)
    copy.start()
    for n in range(4):
        held[source[n]] = pieces[n][: 32 * SLICE_B]
    copy.wait()

    def step(n, count):
        m, at = n // 32, n % 32
        here = flags_s[m, at]
        to = jnp.minimum(count, CAP_B - 1)
        packed[pl.ds(pl.multiple_of(to * SLICE_B, SLICE_B), SLICE_B)] = held[
            m, pl.ds(pl.multiple_of(at * SLICE_B, SLICE_B), SLICE_B)
        ]
        place_s[m, at] = jnp.where(here > 0, to + 1, 0)
        return count + jnp.where(here > 0, 1, 0)

    lax.fori_loop(0, 128, step, jnp.int32(0), unroll=8)
    copy = pltpu.make_async_copy(place_s, flags_v, sem)
    copy.start()
    copy.wait()
    lane = lax.broadcasted_iota(jnp.int32, (SLICE, WIDTH), 1)
    place = flags_v[...].astype(jnp.float32)
    place = jnp.where((lane < 32) & (lax.broadcasted_iota(jnp.int32, (SLICE, WIDTH), 0) < 4), jnp.concatenate([place, place], axis=0), jnp.float32(0.0))
    in_a = jnp.zeros((SLICE, WIDTH), jnp.float32)
    sub = lax.broadcasted_iota(jnp.int32, (SLICE, WIDTH), 0)
    for m in range(8):
        row = pieces_a[PIECE * m + 32 * SLICE : PIECE * (m + 1)].astype(jnp.float32)
        in_a += row
        place = jnp.where((lane >= 32) & (lane < 64) & (sub == m), row, place)
    counts = []
    for pair in range(2):
        one, two = slots[2 * pair] * 8, slots[2 * pair + 1] * 8
        counted = ((lane >= one) & (lane < one + 8)) | ((lane >= two) & (lane < two + 8))
        counts.append(jnp.sum(jnp.where(counted & (sub == 0), in_a, jnp.float32(0.0))))
    over = jnp.where(jnp.maximum(counts[0], counts[1]) > CAP, jnp.float32(1.0), jnp.float32(0.0))
    packed[HEADER_B:PACKED_B] = jnp.where(sub < 8, place, over).astype(jnp.bfloat16)


def pack_b(pieces, source, pieces_a, slots):
    return pl.pallas_call(
        pack_b_kernel,
        in_specs=[space(pltpu.SMEM)] * 2 + [space(pltpu.VMEM)] * 5,
        out_specs=space(pltpu.VMEM),
        out_shape=jax.ShapeDtypeStruct((PACKED_B, WIDTH), jnp.bfloat16),
        scratch_shapes=[
            pltpu.VMEM((4, 32 * SLICE_B, WIDTH), jnp.bfloat16),
            pltpu.VMEM((8, WIDTH), jnp.int32),
            pltpu.SMEM((8, WIDTH), jnp.int32),
            pltpu.SMEM((8, WIDTH), jnp.int32),
            pltpu.SemaphoreType.DMA,
        ],
    )(source, slots, *pieces, pieces_a)


def over_capacity(panel):
    sub = lax.broadcasted_iota(jnp.int32, (SLICE, WIDTH), 0)
    lane = lax.broadcasted_iota(jnp.int32, (SLICE, WIDTH), 1)
    most_a, most_b = jnp.zeros((SLICE, WIDTH), jnp.float32), jnp.zeros((SLICE, 1), jnp.float32)
    for ring in range(4):
        count = jnp.zeros((SLICE, WIDTH), jnp.float32)
        for m in range(4):
            at = (m * 4 + ring) * PACKED_B + HEADER_B
            header = panel[at : at + SLICE].astype(jnp.float32)
            count += header
            most_a = jnp.maximum(most_a, header)
        count = jnp.where((lane >= 32) & (lane < 64) & (sub < 8), count, jnp.float32(0.0))
        most_b = jnp.maximum(most_b, jnp.sum(count, axis=1, keepdims=True))
    most_a = jnp.max(jnp.where(sub == 8, most_a, jnp.float32(0.0)))
    return ((most_a > 0) | (jnp.max(most_b) > CAP_B - 1)).astype(jnp.int32)


def product_kernel(source, slots, *refs):
    panel, out, over = refs[10:13]
    header_v, header_s, listed, rhs, lhs, total, sem = refs[13:]
    over[0] = over_capacity(panel)
    parts = [
        [[(r[0], dy * PACKED), (r[1], dy * PACKED), (r[3 + dy], 0), (r[2], dy * PACKED)] for dy in range(2)]
        for r in (refs[:5], refs[5:10])
    ]
    for pair in range(2):
        at = CAP * SLICE
        header_v[pair * SLICE : (pair + 1) * SLICE] = parts[pair][0][0][0][at : at + SLICE].astype(jnp.float32).astype(jnp.int32)
    for n in range(4):
        at = n * PACKED_B + HEADER_B
        header_v[(2 + n) * SLICE : (3 + n) * SLICE] = panel[at : at + SLICE].astype(jnp.float32).astype(jnp.int32)
    copy = pltpu.make_async_copy(header_v, header_s, sem)
    copy.start()
    copy.wait()

    length = jnp.int32(0)
    chunks = []
    for pair in range(2):
        q0, q1 = slots[2 * pair], slots[2 * pair + 1]

        def step(k, length, pair=pair, q0=q0, q1=q1):
            first = header_s[pair * SLICE + k // 8, q0 * 8 + k % 8]
            second = header_s[pair * SLICE + k // 8, q1 * 8 + k % 8]
            listed[0, length] = k
            listed[1, length] = first
            listed[2, length] = second
            return length + jnp.where(first + second > 0, 1, 0)

        length = lax.fori_loop(0, 64, step, length, unroll=8)
        for i in range(CHUNK - 1):
            for n in range(3):
                listed[n, length + i] = 0
        length = (length + CHUNK - 1) // CHUNK * CHUNK
        chunks.append(length // CHUNK)
    total[...] = jnp.zeros_like(total)

    def multiply(chunk, carry, pair):
        for i in range(CHUNK):
            for slot in range(2):
                place = listed[1 + slot, chunk * CHUNK + i]
                at = jnp.maximum(place - 1, 0) * SLICE
                for dy in range(2):
                    for step in range(4):
                        part, begin = parts[pair][dy][step]
                        value = part[pl.ds(pl.multiple_of(at + begin, SLICE), SLICE)]
                        rows = pl.ds(pl.multiple_of(slot * WIDTH + source[dy * 4 + step] * SLICE, SLICE), SLICE)
                        lhs[rows, i * WIDTH : (i + 1) * WIDTH] = jnp.where(place > 0, value, jnp.zeros_like(value))
            k = listed[0, chunk * CHUNK + i]
            ring = k // 4 % 4
            for j in range(8):
                place = header_s[(2 + ring) * SLICE + k // 16, k % 4 * 8 + j]
                at = ring * PACKED_B + jnp.maximum(place - 1, 0) * SLICE_B
                for m in range(4):
                    value = panel[pl.ds(pl.multiple_of(at + m * 4 * PACKED_B, SLICE), SLICE_B)]
                    rhs[i * WIDTH + m * SLICE_B : i * WIDTH + (m + 1) * SLICE_B, j * WIDTH : (j + 1) * WIDTH] = jnp.where(
                        place > 0, value, jnp.zeros_like(value)
                    )
        for n in range(4):
            cols = slice(n * 256, (n + 1) * 256)
            total[pair, :, cols] += jnp.dot(lhs[...], rhs[:, cols], preferred_element_type=jnp.float32)
        return carry

    lax.fori_loop(0, chunks[0], functools.partial(multiply, pair=0), 0)
    lax.fori_loop(chunks[0], chunks[1], functools.partial(multiply, pair=1), 0)
    for slot in range(4):
        q = slots[slot]
        rows = slice(slot % 2 * WIDTH, (slot % 2 + 1) * WIDTH)
        for j in range(8):
            block = total[slot // 2, rows, j * WIDTH : (j + 1) * WIDTH]
            out[slot * WIDTH : (slot + 1) * WIDTH, j * WIDTH : (j + 1) * WIDTH] = jnp.where(
                header_s[slot // 2 * SLICE + 8, q * 8 + j] > 0, block, jnp.zeros_like(block)
            ).astype(jnp.bfloat16)


def packed_product(parts, panel, source, slots):
    return pl.pallas_call(
        product_kernel,
        in_specs=[space(pltpu.SMEM)] * 2 + [space(pltpu.VMEM)] * 11,
        out_specs=[space(pltpu.VMEM), space(pltpu.SMEM)],
        out_shape=[jax.ShapeDtypeStruct((512, 1024), jnp.bfloat16), jax.ShapeDtypeStruct((1,), jnp.int32)],
        scratch_shapes=[
            pltpu.VMEM((6 * SLICE, WIDTH), jnp.int32),
            pltpu.SMEM((6 * SLICE, WIDTH), jnp.int32),
            pltpu.SMEM((3, 2 * 64 + 2 * CHUNK), jnp.int32),
            pltpu.VMEM((CHUNK * WIDTH, 1024), jnp.bfloat16),
            pltpu.VMEM((2 * WIDTH, CHUNK * WIDTH), jnp.bfloat16),
            pltpu.VMEM((2, 2 * WIDTH, 1024), jnp.float32),
            pltpu.SemaphoreType.DMA,
        ],
        compiler_params=pltpu.CompilerParams(vmem_limit_bytes=24 * 2**20),
    )(source, slots, *parts, panel)


def dense_product(a, b, a_pattern, b_pattern, c_pattern, slots, slot_shift, source, row):
    value = masked(a, a_pattern)
    moved, kept = [], []
    for pair in range(2):
        rows = [lax.dynamic_slice_in_dim(value, slots[2 * pair + t] * WIDTH, WIDTH, 0) for t in range(2)]
        flags = [lax.dynamic_slice_in_dim(c_pattern, slots[2 * pair + t], 1, 0) for t in range(2)]
        moved.append(shifted(jnp.concatenate(rows, axis=0), ROW, 16, slot_shift[2 * pair]))
        kept.append(shifted(jnp.concatenate(flags, axis=0), ROW, 16, slot_shift[2 * pair]))
    value = jnp.concatenate(moved, axis=0)
    full = jnp.zeros((512, 8192), jnp.bfloat16)
    for t, offset in enumerate(OFFSETS):
        piece = from_offset(value, offset) if t else value
        full = lax.dynamic_update_slice(full, piece, (0, source[t] * 1024))
    own_b = masked(b, b_pattern)
    panel = jnp.zeros((8192, 1024), jnp.bfloat16)
    for by in range(16):
        piece = lax.ppermute(own_b, ROW, [((i + by) % 16, i) for i in range(16)]) if by else own_b
        panel = lax.dynamic_update_slice(panel, piece, ((row + by) % 16 * 512, 0))
    product = jnp.dot(full, panel, preferred_element_type=jnp.float32)
    mask = jnp.repeat(jnp.repeat(jnp.concatenate(kept, axis=0), WIDTH, axis=0), WIDTH, axis=1)
    return jnp.where(mask > 0, product, jnp.float32(0.0)).astype(jnp.bfloat16)


def local(a, b, a_pattern, b_pattern, c_pattern, owner_list):
    slot_shift = owner_list[:4] // 4 % 16
    slots = owner_list[:4] % 4
    yh, z = lax.axis_index("yh").astype(jnp.int32), lax.axis_index("z").astype(jnp.int32)
    row = lax.axis_index(ROW).astype(jnp.int32)
    ahead = jnp.stack([(yh + dy) % 2 * 4 + (z + dz) % 4 for dy, dz in OFFSETS])
    cut_a = cut(a, a_pattern, b_pattern)
    b_after, _ = lax.optimization_barrier((b, cut_a))
    pieces_a = lax.all_to_all(cut_a, COL, 0, 0, tiled=True)
    x = lax.axis_index("x").astype(jnp.int32)
    pieces_b = cut_b(b_after, b_pattern, jnp.stack([(x - n) % 4 for n in range(4)]))
    pieces_b = [from_ahead(piece, "x", n) if n else piece for n, piece in enumerate(pieces_b)]
    first, second = pack_a(pieces_a, slots, c_pattern)
    pieces_b, _ = lax.optimization_barrier((pieces_b, first))
    packed_b = pack_b(pieces_b, jnp.stack([(x + n) % 4 for n in range(4)]), pieces_a, slots)
    panel = lax.all_gather(packed_b, ROW, axis=0, tiled=True)
    parts = []
    for pair, packed in enumerate((first, second)):
        moved = shifted(packed, ROW, 16, slot_shift[2 * pair])
        both = jnp.concatenate([moved, from_ahead(moved, "yh", 1)], axis=0)
        near = [from_ahead(both, "z", step) for step in (1, 3)]
        far = [from_ahead(near[0][:PACKED], "z", 1), from_ahead(near[1][PACKED:], "z", 3)]
        parts += [both, *near, *far]
    product, over = packed_product(parts, panel, ahead, slots)
    return lax.cond(
        over[0] > 0,
        lambda: dense_product(a, b, a_pattern, b_pattern, c_pattern, slots, slot_shift, ahead, row),
        lambda: product,
    )


def solution(mesh):
    fine = Mesh(mesh.devices.reshape(tuple(SIZES.values())), tuple(SIZES))
    return jax.shard_map(
        local,
        mesh=fine,
        in_specs=(P(ROW, COL),) * 5 + (P(),),
        out_specs=P(ROW, COL),
        check_vma=False,
    )
```
